768 devices in a mesh: row: 24 (over x, z_lo, core), col: 32 (over z_hi, y).
Axes of the slice: x: 4, y: 8, z: 12 (z_hi: 4, z_lo: 3; z = z_hi * 3 + z_lo), core: 2. Of those that a mesh axis runs over, the one named last changes fastest.
Arguments:
- vectors: bfloat16 [1, 16, 24576], P(None, None, ('col', 'row')), may hold values from -110 to 110
- h_tiles: bfloat16 [1, 24, 1024, 128, 128], P(None, 'row', 'col'), may hold values from -0.0625 to 0.0625
- h_list: int32 [1, 24, 1024], P(None, 'row', 'col'), may hold values from -1 to 47, as said below
- j_tiles: bfloat16 [1, 24, 384, 128, 128], P(None, 'row', 'col'), may hold values from -0.109375 to 0.109375
- j_list: int32 [1, 24, 384], P(None, 'row', 'col'), may hold values from -1 to 95, as said below
Outputs:
- basis: float32 [1, 16, 24576], P(None, None, ('row', 'col'))
- transitions: float32 [1, 2, 16, 16], replicated
The draws below stay inside these ranges and needn't reach their ends.
Inputs may be any that keep to these rules, and one draw needn't show every extreme that they name: `h_list`: each block's 32 entries list distinct tile positions first and then -1; at most 32 positions a block, and some block lists all 32. `j_list`: each block's 12 entries list distinct codes first and then -1; at most 12 codes a block, and some block lists all 12.
All inputs are finite; a program needn't handle non-finite values.
Results may differ from the reference program's by a relative error of at most 0.0003.
Values may be sent and summed in bfloat16 or wider, within the bound.
A program may use at most 64 MiB of HBM per device.

```python
import math
import jax
import jax.numpy as jnp
from jax import lax

K = 16
TILE = 128
RT = 8
SECT = 1
HSLOT = 32
JSLOT = 12
NSIT = 6
NS = 24576
CT = 6
N_ROW = 24
N_COL = 32


def listed_codes(key, slot_count, position_count):
    block_count = SECT * N_ROW * N_COL
    key_order, key_count, key_full, key_pick = jax.random.split(key, 4)
    orders = jax.vmap(lambda single: jax.random.permutation(single, position_count))(jax.random.split(key_order, block_count))
    sparse_count = jax.random.randint(key_count, (block_count,), slot_count // 4, slot_count // 2 + 1)
    filled = jax.random.randint(key_full, (block_count,), 0, 8) == 0
    chosen = jax.random.randint(key_pick, (), 0, block_count)
    counts = jnp.where(filled | (jnp.arange(block_count) == chosen), slot_count, sparse_count)
    codes = jnp.where(jnp.arange(slot_count)[None, :] < counts[:, None], orders[:, :slot_count], -1)
    return codes.reshape(SECT, N_ROW, N_COL * slot_count).astype(jnp.int32)


def draw_h_list(key, part):
    return listed_codes(jax.random.fold_in(key, 11), HSLOT, RT * CT)


def draw_j_list(key, part):
    return listed_codes(jax.random.fold_in(key, 23), JSLOT, 2 * RT * CT)


def draw_vectors(key, part):
    key_noise, key_common, key_scale = jax.random.split(jax.random.fold_in(key, 37), 3)
    noise_part = jnp.clip(jax.random.normal(key_noise, (SECT, K, NS), jnp.float32), -4.0, 4.0)
    common = jnp.clip(jax.random.normal(key_common, (SECT, 1, NS), jnp.float32), -4.0, 4.0)
    mixing = 0.7
    spread = math.log(10.0)
    column_scale = jnp.exp(jax.random.uniform(key_scale, (SECT, K, 1), jnp.float32) * spread)
    row_scale = 0.5 + jnp.arange(NS, dtype=jnp.float32) / NS
    return (column_scale * row_scale * (noise_part + mixing * common)).astype(jnp.bfloat16)


def shard_levels(stream_key, dims, pieces, smallest, largest):
    level, own = 1.0, jax.random.fold_in(stream_key, 6)
    for axis_at, shards_of in pieces:
        draws = jnp.exp(jax.random.uniform(jax.random.fold_in(own, axis_at), (shards_of,), jnp.float32, smallest / len(pieces), largest / len(pieces)))
        level = level * jnp.repeat(draws, dims[axis_at] // shards_of).reshape([-1 if axis == axis_at else 1 for axis in range(len(dims))])
    return level


def gaussian(own_key, shape, width, reach, shards=(), held_as=jnp.bfloat16):
    gain = shard_levels(own_key, shape, shards, -0.22, 0.18) if shards else 1.0
    entries = jax.random.normal(own_key, shape, jnp.float32) * width * gain
    return jnp.minimum(jnp.maximum(entries, -reach), reach).astype(held_as)


def setup_inputs(seed: int = 0) -> dict:
    arg_keys = jax.random.split(jax.random.key(seed), 6)
    vectors = draw_vectors(jax.random.fold_in(arg_keys[5], 71), 0)
    h_tiles = gaussian(arg_keys[1], (SECT, N_ROW, N_COL * HSLOT, TILE, TILE), (NS // 3) ** -0.5, 0.0625, ((1, 24), (2, 32)))
    h_list = draw_h_list(jax.random.fold_in(arg_keys[5], 71), 0)
    j_tiles = gaussian(arg_keys[3], (SECT, N_ROW, N_COL * JSLOT, TILE, TILE), (NS // 8) ** -0.5, 0.109375, ((1, 24), (2, 32)))
    j_list = draw_j_list(jax.random.fold_in(arg_keys[5], 71), 0)
    return {"vectors": vectors, "h_tiles": h_tiles, "h_list": h_list, "j_tiles": j_tiles, "j_list": j_list}


exact_precision = lax.Precision.HIGHEST

def tile_products(tile_data, code_data, vector_set, operator_count):
    slot_count = code_data.shape[1] // N_COL
    position_count = RT * CT
    column_vectors = vector_set.reshape(K, N_COL, CT, TILE).astype(jnp.float32)

    def one_row(inputs):
        tile_row, code_row = inputs
        tile_row = tile_row.reshape(N_COL, slot_count, TILE, TILE).astype(jnp.float32)
        code_row = code_row.reshape(N_COL, slot_count)
        places = code_row % position_count
        operator = code_row // position_count
        column_hot = (places[:, :, None] % CT == jnp.arange(CT)[None, None, :]).astype(jnp.float32)
        picked = jnp.einsum('jqc,kjcb->jqkb', column_hot, column_vectors, precision=exact_precision)
        product = jnp.einsum('jqab,jqkb->jqka', tile_row, picked, precision=exact_precision)
        row_hot = ((operator[:, :, None, None] == jnp.arange(operator_count)[None, None, :, None]) & (places[:, :, None, None] // CT == jnp.arange(RT)[None, None, None, :]) & (code_row[:, :, None, None] >= 0)).astype(jnp.float32)
        result = jnp.einsum('jqor,jqka->okra', row_hot, product, precision=exact_precision)
        return result.reshape(operator_count, K, RT * TILE)
    stacked = lax.map(one_row, (tile_data, code_data))
    return stacked.transpose(1, 2, 0, 3).reshape(operator_count, K, NS)

def orthonormal_root(gram):
    scale = jnp.sqrt(jnp.sum(gram * gram) + 1e-06)
    iterate = gram / scale
    identity = jnp.eye(K, dtype=jnp.float32)
    inverse_root = identity
    for iteration in range(NSIT):
        middle = 1.5 * identity - 0.5 * jnp.dot(inverse_root, iterate, precision=exact_precision)
        iterate = jnp.dot(iterate, middle, precision=exact_precision)
        inverse_root = jnp.dot(middle, inverse_root, precision=exact_precision)
    return (inverse_root, scale)

def reference(vectors, h_tiles, h_list, j_tiles, j_list):
    basis_list = []
    transition_list = []
    for sector in range(SECT):
        projected = tile_products(h_tiles[sector], h_list[sector], vectors[sector], 1)[0]
        applied = tile_products(j_tiles[sector], j_list[sector], vectors[sector], 2)
        gram = jnp.einsum('kp,lp->kl', projected, projected, precision=exact_precision)
        inverse_root, scale = orthonormal_root(gram)
        basis = jnp.sqrt(NS / scale) * jnp.einsum('mk,mp->kp', inverse_root, projected, precision=exact_precision)
        elements = jnp.einsum('kp,alp->akl', basis, applied, precision=exact_precision) / math.sqrt(NS)
        basis_list.append(basis)
        transition_list.append(elements)
    return (jnp.stack(basis_list), jnp.stack(transition_list))
```

```python
import functools

import jax
import jax.numpy as jnp
from jax import lax
from jax.experimental import pallas as pl
from jax.experimental.pallas import tpu as pltpu
from jax.sharding import PartitionSpec as P

NSIT = 6
MESH = pl.DeviceIdType.MESH
F32 = jnp.float32
BF16 = jnp.bfloat16
NY = 8
NZ = 4
K = 16
T = 128
NT = (((1,), (1,)), ((), ()))


def iota(shape, dim):
    return lax.broadcasted_iota(jnp.int32, shape, dim)


def three_parts(x):
    a = x.astype(BF16).astype(F32)
    rest = x - a
    b = rest.astype(BF16).astype(F32)
    return a, b, rest - b


def small_dot(left, right, group):
    a1, a2, a3 = three_parts(left)
    b1, b2, b3 = (b.astype(BF16) for b in three_parts(right))
    lhs = jnp.where(
        (group == 0) | (group == 1) | (group == 4),
        a1,
        jnp.where((group == 5) | (group == 7), a3, a2),
    )
    rhs = jnp.concatenate([b1, b2, b1, b2, b3, b1, b3, b2], axis=0)
    return jnp.dot(lhs.astype(BF16), rhs, preferred_element_type=F32)


def long_dot(left, right):
    return lax.dot_general(
        left, right, NT, precision=lax.Precision.HIGHEST, preferred_element_type=F32
    )


def flat_rows(repeated):
    own = iota((8, T), 1) // K == iota((8, T), 0)
    return [
        jnp.sum(jnp.where(own, repeated[8 * h : 8 * h + 8], 0.0), axis=0, keepdims=True)
        for h in range(2)
    ]


def from_flat(rows):
    own = iota((8, T), 1) // K == iota((8, T), 0)
    full = jnp.concatenate(
        [jnp.where(own, jnp.broadcast_to(row, (8, T)), 0.0) for row in rows], axis=0
    )
    for shift in (64, 32, 16):
        full = full + pltpu.roll(full, shift, 1)
    return full


def kernel(
    n_row, n_col, total_rows,
    vec_hbm, ht_hbm, hl, jt_hbm, jl, basis_ref, elem_ref,
    vloc, vsend, vrecv, vblk, ht, jt, hs, hr, js, jr, zr, gs, ga, gb, cs, ca, cb, ps,
    lsem, ssem, rsem,
):
    me_r = lax.axis_index("row")
    me_c = lax.axis_index("col")
    zh = me_c // NY
    y = me_c % NY
    barrier = pltpu.get_barrier_semaphore()

    def at_row(d):
        return {"row": lax.rem(me_r + d, n_row)}

    def at_col(d):
        return {"col": lax.rem(me_c + d, n_col)}

    def at_y(d):
        return {"col": zh * NY + lax.rem(y + d, NY)}

    def at_z(d):
        return {"col": lax.rem(zh + d, NZ) * NY + y}

    loads = [
        pltpu.make_async_copy(vec_hbm, vloc, lsem.at[0]),
        pltpu.make_async_copy(ht_hbm, ht, lsem.at[1]),
        pltpu.make_async_copy(jt_hbm, jt, lsem.at[2]),
    ]
    for load in loads:
        load.start()

    def greet(where):
        def step(d, carry):
            pl.semaphore_signal(barrier, inc=1, device_id=where(d), device_id_type=MESH)
            return carry
        return step

    lax.fori_loop(1, n_row, greet(at_row), 0)
    lax.fori_loop(1, n_col, greet(at_col), 0)

    def send_all(at, where, count, src, dst):
        def step(d, carry):
            pltpu.make_async_remote_copy(
                src_ref=src(d), dst_ref=dst, send_sem=ssem.at[at], recv_sem=rsem.at[at],
                device_id=where(d), device_id_type=MESH,
            ).start()
            return carry
        lax.fori_loop(1, count, step, 0)

    def wait_for(sem, at, buf, count):
        part = buf.at[pl.ds(0, count)]
        pltpu.make_async_copy(part, part, sem.at[at]).wait()

    loads[0].wait()
    place = (iota((32, T), 1) == iota((32, T), 0) + 32 * lax.rem(me_r, 4)).astype(F32).astype(BF16)
    mine = jnp.dot(vloc[0], place, preferred_element_type=F32).astype(BF16)
    vsend[...] = mine
    vrecv[me_r] = mine

    pl.semaphore_wait(barrier, n_row + n_col - 2)
    send_all(0, at_row, n_row, lambda d: vsend, vrecv.at[me_r])
    loads[1].wait()
    loads[2].wait()
    wait_for(rsem, 0, vrecv, n_row - 1)

    for c in range(6):
        block = (vrecv[4 * c].astype(F32) + vrecv[4 * c + 1].astype(F32)) + (
            vrecv[4 * c + 2].astype(F32) + vrecv[4 * c + 3].astype(F32)
        )
        vblk[c] = block

    def masked(code, blocks):
        m = lax.shift_right_arithmetic(code * 43, 8)
        picked = vblk[code - 6 * m]
        which = jnp.full((K, T), m, jnp.int32)
        return jnp.concatenate(
            [jnp.where(which == b, picked, 0.0).astype(BF16) for b in range(blocks)], axis=0
        )

    def products(codes, tiles, count, blocks):
        total = jnp.zeros((blocks * K, T), F32)
        for q in range(0, count, 2):
            left = jnp.concatenate([masked(codes[q + e], blocks) for e in range(2)], axis=1)
            right = jnp.concatenate([tiles[q + e] for e in range(2)], axis=1)
            total = total + lax.dot_general(left, right, NT, preferred_element_type=F32)
        return total

    lane32 = iota((K, T), 1) // 32

    def packed(total, first, yh, s):
        out = None
        for z in range(NZ):
            at = (first + 2 * z + yh) * K
            piece = total[at : at + K]
            shift = ((z - s) % NZ) * 32
            if shift:
                piece = pltpu.roll(piece, shift, 1)
            out = piece if out is None else jnp.where(lane32 == z, piece, out)
        return out

    h_total = products(hl, ht, hl.shape[0], 8)
    for yh in range(2):
        for s in range(4):
            hs[yh * 4 + s] = packed(h_total, 0, yh, s)
    hr[y] = hs[y]
    send_all(1, at_y, NY, lambda d: hs.at[lax.rem(y + d, NY)], hr.at[y])

    j_total = products(jl, jt, jl.shape[0], 16)
    for yh in range(2):
        for s in range(4):
            for o in range(2):
                js[yh * 4 + s, o * K : o * K + K] = packed(j_total, o * 8, yh, s)
    jr[y] = js[y]
    send_all(2, at_y, NY, lambda d: js.at[lax.rem(y + d, NY)], jr.at[y])

    wait_for(rsem, 1, hr, NY - 1)
    part = hr[0]
    for d in range(1, NY):
        part = part + hr[d]
    zr[zh] = part
    send_all(3, at_z, NZ, lambda d: zr.at[zh], zr.at[zh])
    wait_for(rsem, 3, zr, NZ - 1)
    proj = (zr[0] + zr[1]) + (zr[2] + zr[3])

    rows = flat_rows(long_dot(proj, jnp.concatenate([proj] * 8, axis=0)))
    for h in range(2):
        gs[h : h + 1] = rows[h]
        ga[y, h : h + 1] = rows[h]
    send_all(4, at_y, NY, lambda d: gs, ga.at[y])
    own_lanes = proj
    for z in range(1, NZ):
        own_lanes = jnp.where(jnp.full((K, T), zh, jnp.int32) == z, pltpu.roll(proj, (NZ - z) * 32, 1), own_lanes)
    ps[...] = own_lanes

    wait_for(rsem, 2, jr, NY - 1)
    share = jr[0]
    for d in range(1, NY):
        share = share + jr[d]
    for o in range(2):
        rows = flat_rows(long_dot(proj, jnp.concatenate([share[o * K : o * K + K]] * 8, axis=0)))
        for h in range(2):
            cs[2 * o + h : 2 * o + h + 1] = rows[h]
            ca[me_c, 2 * o + h : 2 * o + h + 1] = rows[h]
    send_all(5, at_col, n_col, lambda d: cs, ca.at[me_c])

    wait_for(rsem, 4, ga, NY - 1)
    part = ga[0]
    for d in range(1, NY):
        part = part + ga[d]
    gb[me_r] = part
    send_all(6, at_row, n_row, lambda d: gb.at[me_r], gb.at[me_r])

    wait_for(rsem, 5, ca, n_col - 1)
    part = ca[0]
    for d in range(1, n_col):
        part = part + ca[d]
    cb[me_r] = part
    send_all(7, at_row, n_row, lambda d: cb.at[me_r], cb.at[me_r])

    wait_for(rsem, 6, gb, n_row - 1)
    part = gb[0]
    for d in range(1, n_row):
        part = part + gb[d]
    square = jnp.sum(jnp.sum(part * part, axis=1, keepdims=True), axis=0, keepdims=True)
    scale = jnp.sqrt(jnp.broadcast_to(square, (K, T)) + 1e-06)
    iterate = from_flat([part[0:1], part[1:2]]) / scale
    group = iota((K, T), 1) // K
    identity = (iota((K, T), 1) % K == iota((K, T), 0)).astype(F32)
    middle = 1.5 * identity - 0.5 * iterate
    iterate = small_dot(middle, iterate, group)
    root = middle
    for step in range(1, NSIT):
        middle = 1.5 * identity - 0.5 * small_dot(iterate, root, group)
        if step < NSIT - 1:
            iterate = small_dot(middle, iterate, group)
        root = small_dot(root, middle, group)
    basis = jnp.sqrt(total_rows / scale) * small_dot(root, ps[...], group)
    basis_ref[0] = basis[:, :32]

    wait_for(rsem, 7, cb, n_row - 1)
    part = cb[0]
    for d in range(1, n_row):
        part = part + cb[d]
    for o in range(2):
        cross = from_flat([part[2 * o : 2 * o + 1], part[2 * o + 1 : 2 * o + 2]])
        elements = small_dot(root, cross, group) / jnp.sqrt(scale)
        elem_ref[0, o] = elements[:, :K]

    wait_for(ssem, 0, vrecv, n_row - 1)
    wait_for(ssem, 1, hr, NY - 1)
    wait_for(ssem, 2, jr, NY - 1)
    wait_for(ssem, 3, zr, NZ - 1)
    wait_for(ssem, 4, ga, NY - 1)
    wait_for(ssem, 5, ca, n_col - 1)
    wait_for(ssem, 6, gb, n_row - 1)
    wait_for(ssem, 7, cb, n_row - 1)


def solution(mesh):
    n_row, n_col = mesh.shape["row"], mesh.shape["col"]

    def per_device(vectors, h_tiles, h_list, j_tiles, j_list):
        hq, jq = h_tiles.shape[2], j_tiles.shape[2]
        total_rows = vectors.shape[2] * n_row * n_col
        hbm = pl.BlockSpec(memory_space=pl.ANY)
        smem = pl.BlockSpec(memory_space=pltpu.SMEM)
        vmem = pl.BlockSpec(memory_space=pltpu.VMEM)
        return pl.pallas_call(
            functools.partial(kernel, n_row, n_col, float(total_rows)),
            out_shape=(
                jax.ShapeDtypeStruct((1, K, 32), F32),
                jax.ShapeDtypeStruct((1, 2, K, K), F32),
            ),
            in_specs=[hbm, hbm, smem, hbm, smem],
            out_specs=(vmem, vmem),
            scratch_shapes=[
                pltpu.VMEM((1, K, 32), BF16),
                pltpu.VMEM((K, T), BF16),
                pltpu.VMEM((n_row, K, T), BF16),
                pltpu.VMEM((6, K, T), F32),
                pltpu.VMEM((hq, T, T), BF16),
                pltpu.VMEM((jq, T, T), BF16),
                pltpu.VMEM((NY, K, T), F32),
                pltpu.VMEM((NY, K, T), F32),
                pltpu.VMEM((NY, 2 * K, T), F32),
                pltpu.VMEM((NY, 2 * K, T), F32),
                pltpu.VMEM((NZ, K, T), F32),
                pltpu.VMEM((2, T), F32),
                pltpu.VMEM((NY, 2, T), F32),
                pltpu.VMEM((n_row, 2, T), F32),
                pltpu.VMEM((4, T), F32),
                pltpu.VMEM((n_col, 4, T), F32),
                pltpu.VMEM((n_row, 4, T), F32),
                pltpu.VMEM((K, T), F32),
                pltpu.SemaphoreType.DMA((3,)),
                pltpu.SemaphoreType.DMA((8,)),
                pltpu.SemaphoreType.DMA((8,)),
            ],
            compiler_params=pltpu.CompilerParams(
                collective_id=0, has_side_effects=True, vmem_limit_bytes=24 * 1024 * 1024
            ),
        )(
            vectors,
            h_tiles.reshape(hq, T, T),
            h_list.reshape(hq),
            j_tiles.reshape(jq, T, T),
            j_list.reshape(jq),
        )

    return jax.shard_map(
        per_device,
        mesh=mesh,
        in_specs=(
            P(None, None, ("col", "row")),
            P(None, "row", "col", None, None),
            P(None, "row", "col"),
            P(None, "row", "col", None, None),
            P(None, "row", "col"),
        ),
        out_specs=(P(None, None, ("row", "col")), P()),
        check_vma=False,
    )
```

```python
import functools

import jax
import jax.numpy as jnp
from jax import lax
from jax.experimental import pallas as pl
from jax.experimental.pallas import tpu as pltpu
from jax.sharding import PartitionSpec as P

NSIT = 6
MESH = pl.DeviceIdType.MESH
F32 = jnp.float32
BF16 = jnp.bfloat16
NY = 8
NZ = 4
NX = 4
VEC, HY, JY, HZ, JZ, PZ, GA, CA, GB, CB = range(10)
K = 16
T = 128
NT = (((1,), (1,)), ((), ()))


def iota(shape, dim):
    return lax.broadcasted_iota(jnp.int32, shape, dim)


def three_parts(x):
    a = x.astype(BF16).astype(F32)
    rest = x - a
    b = rest.astype(BF16).astype(F32)
    return a, b, rest - b


def small_dot(left, right, group):
    a1, a2, a3 = three_parts(left)
    b1, b2, b3 = (b.astype(BF16) for b in three_parts(right))
    lhs = jnp.where(
        (group == 0) | (group == 1) | (group == 4),
        a1,
        jnp.where((group == 5) | (group == 7), a3, a2),
    )
    rhs = jnp.concatenate([b1, b2, b1, b2, b3, b1, b3, b2], axis=0)
    return jnp.dot(lhs.astype(BF16), rhs, preferred_element_type=F32)


def long_dot(left, right):
    return lax.dot_general(
        left, right, NT, precision=lax.Precision.HIGHEST, preferred_element_type=F32
    )


def flat_rows(repeated):
    own = iota((8, T), 1) // K == iota((8, T), 0)
    return [
        jnp.sum(jnp.where(own, repeated[8 * h : 8 * h + 8], 0.0), axis=0, keepdims=True)
        for h in range(2)
    ]


def from_flat(rows):
    own = iota((8, T), 1) // K == iota((8, T), 0)
    full = jnp.concatenate(
        [jnp.where(own, jnp.broadcast_to(row, (8, T)), 0.0) for row in rows], axis=0
    )
    for shift in (64, 32, 16):
        full = full + pltpu.roll(full, shift, 1)
    return full


def kernel(
    n_row, n_col, total_rows,
    vec_hbm, ht_hbm, hl_hbm, jt_hbm, jl_hbm, basis_ref, elem_ref,
    vloc, vsend, vrecv, vblk, ht, jt, hl, jl, hs, hr, js, jr, hz, jz, pz, gs, ga, gb, cs, ca, cb,
    lsem, ssem, rsem,
):
    me_r = lax.axis_index("row")
    me_c = lax.axis_index("col")
    zh = me_c // NY
    y = me_c % NY
    x = me_r // (n_row // NX)
    inner = me_r % (n_row // NX)
    n_in = n_row // NX
    last = NZ - 1
    at_last = zh == last
    barrier = pltpu.get_barrier_semaphore()

    def wrap(value, count):
        return jnp.where(value >= count, value - count, value)

    def at_row(d):
        return {"row": wrap(me_r + d, n_row)}

    def at_y(d):
        return {"col": zh * NY + wrap(y + d, NY)}

    def at_z(d):
        return {"col": wrap(zh + d, NZ) * NY + y}

    def at_plane(d):
        to = y * NX + x + d
        to = wrap(to, NX * NY)
        return {"row": (to % NX) * n_in + inner, "col": zh * NY + to // NX}

    def at_line(d):
        to = wrap(zh * n_in + inner + d, NZ * n_in)
        return {"row": x * n_in + to % n_in, "col": (to // n_in) * NY + y}

    def at_collector(d):
        return {"col": last * NY + y}

    codes = [
        pltpu.make_async_copy(hl_hbm, hl, lsem.at[3]),
        pltpu.make_async_copy(jl_hbm, jl, lsem.at[4]),
    ]
    loads = [
        pltpu.make_async_copy(vec_hbm, vloc, lsem.at[0]),
        pltpu.make_async_copy(ht_hbm, ht, lsem.at[1]),
        pltpu.make_async_copy(jt_hbm, jt, lsem.at[2]),
    ]

    def greet(where):
        def step(d, carry):
            pl.semaphore_signal(barrier, inc=1, device_id=where(d), device_id_type=MESH)
            return carry
        return step

    def send_all(at, where, count, src, dst):
        def step(d, carry):
            pltpu.make_async_remote_copy(
                src_ref=src(d), dst_ref=dst, send_sem=ssem.at[at], recv_sem=rsem.at[at],
                device_id=where(d), device_id_type=MESH,
            ).start()
            return carry
        lax.fori_loop(1, count + 1, step, 0)

    def wait_for(sem, at, buf, count):
        part = buf.at[pl.ds(0, count)]
        pltpu.make_async_copy(part, part, sem.at[at]).wait()

    def total_of(buf, count):
        parts = [buf[d] for d in range(count)]
        while len(parts) > 1:
            parts = [sum(parts[k + 1 : k + 2], parts[k]) for k in range(0, len(parts), 2)]
        return parts[0]

    lax.fori_loop(1, n_row, greet(at_row), 0)
    lax.fori_loop(1, NY, greet(at_y), 0)
    lax.fori_loop(1, NZ, greet(at_z), 0)
    for load in [loads[0]] + codes + loads[1:]:
        load.start()
    loads[0].wait()
    place = (iota((32, T), 1) == iota((32, T), 0) + 32 * lax.rem(me_r, 4)).astype(F32).astype(BF16)
    mine = jnp.dot(vloc[0], place, preferred_element_type=F32).astype(BF16)
    vsend[...] = mine
    vrecv[me_r] = mine
    for load in codes:
        load.wait()

    pl.semaphore_wait(barrier, n_row - 1 + NY - 1 + NZ - 1)
    send_all(VEC, at_row, n_row - 1, lambda d: vsend, vrecv.at[me_r])
    loads[1].wait()
    loads[2].wait()
    wait_for(rsem, VEC, vrecv, n_row - 1)

    for c in range(6):
        block = (vrecv[4 * c].astype(F32) + vrecv[4 * c + 1].astype(F32)) + (
            vrecv[4 * c + 2].astype(F32) + vrecv[4 * c + 3].astype(F32)
        )
        vblk[c] = block

    def masked(code, blocks):
        m = lax.shift_right_arithmetic(code * 43, 8)
        picked = vblk[code - 6 * m]
        which = jnp.full((K, T), m, jnp.int32)
        return jnp.concatenate(
            [jnp.where(which == b, picked, 0.0).astype(BF16) for b in range(blocks)], axis=0
        )

    def products(codes, tiles, count, blocks):
        total = jnp.zeros((blocks * K, T), F32)
        for q in range(0, count, 2):
            left = jnp.concatenate([masked(codes[0, 0, q + e], blocks) for e in range(2)], axis=1)
            right = jnp.concatenate([tiles[q + e] for e in range(2)], axis=1)
            total = total + lax.dot_general(left, right, NT, preferred_element_type=F32)
        return total

    lane32 = iota((K, T), 1) // 32

    def packed(total, first, yh, s):
        out = None
        for z in range(NZ):
            at = (first + 2 * z + yh) * K
            piece = total[at : at + K]
            shift = ((z - s) % NZ) * 32
            if shift:
                piece = pltpu.roll(piece, shift, 1)
            out = piece if out is None else jnp.where(lane32 == z, piece, out)
        return out

    h_total = products(hl, ht, ht.shape[0], 8)
    for yh in range(2):
        for s in range(4):
            hs[yh * 4 + s] = packed(h_total, 0, yh, s)
    hr[y] = hs[y]
    send_all(HY, at_y, NY - 1, lambda d: hs.at[wrap(y + d, NY)], hr.at[y])

    j_total = products(jl, jt, jt.shape[0], 16)
    for yh in range(2):
        for s in range(4):
            for o in range(2):
                js[yh * 4 + s, o * K : o * K + K] = packed(j_total, o * 8, yh, s)
    jr[y] = js[y]
    send_all(JY, at_y, NY - 1, lambda d: js.at[wrap(y + d, NY)], jr.at[y])

    wait_for(rsem, HY, hr, NY - 1)
    hz[zh] = total_of(hr, NY)

    @pl.when(jnp.logical_not(at_last))
    def _():
        send_all(HZ, at_collector, 1, lambda d: hz.at[zh], hz.at[zh])
        wait_for(rsem, JY, jr, NY - 1)
        jz[zh] = total_of(jr, NY)
        send_all(JZ, at_collector, 1, lambda d: jz.at[zh], jz.at[zh])
        wait_for(rsem, PZ, pz, 1)

    @pl.when(at_last)
    def _():
        slot = y * NX + x
        wait_for(rsem, HZ, hz, NZ - 1)
        proj = total_of(hz, NZ)
        pz[0] = proj
        rows = flat_rows(long_dot(proj, jnp.concatenate([proj] * 8, axis=0)))
        for h in range(2):
            gs[h : h + 1] = rows[h]
            ga[slot, h : h + 1] = rows[h]
        send_all(GA, at_plane, NX * NY - 1, lambda d: gs, ga.at[slot])
        send_all(PZ, at_z, NZ - 1, lambda d: pz.at[0], pz.at[0])

        wait_for(rsem, JY, jr, NY - 1)
        jz[zh] = total_of(jr, NY)
        wait_for(rsem, JZ, jz, NZ - 1)
        share = total_of(jz, NZ)
        for o in range(2):
            rows = flat_rows(
                long_dot(proj, jnp.concatenate([share[o * K : o * K + K]] * 8, axis=0))
            )
            for h in range(2):
                cs[2 * o + h : 2 * o + h + 1] = rows[h]
                ca[slot, 2 * o + h : 2 * o + h + 1] = rows[h]
        send_all(CA, at_plane, NX * NY - 1, lambda d: cs, ca.at[slot])

        wait_for(rsem, GA, ga, NX * NY - 1)
        gb[inner] = total_of(ga, NX * NY)
        send_all(GB, at_line, NZ * n_in - 1, lambda d: gb.at[inner], gb.at[inner])
        wait_for(rsem, CA, ca, NX * NY - 1)
        cb[inner] = total_of(ca, NX * NY)
        send_all(CB, at_line, NZ * n_in - 1, lambda d: cb.at[inner], cb.at[inner])
        wait_for(rsem, GB, gb, n_in - 1)

    @pl.when(jnp.logical_not(at_last))
    def _():
        wait_for(rsem, GB, gb, n_in)

    part = total_of(gb, n_in)
    square = jnp.sum(jnp.sum(part * part, axis=1, keepdims=True), axis=0, keepdims=True)
    scale = jnp.sqrt(jnp.broadcast_to(square, (K, T)) + 1e-06)
    iterate = from_flat([part[0:1], part[1:2]]) / scale
    group = iota((K, T), 1) // K
    identity = (iota((K, T), 1) % K == iota((K, T), 0)).astype(F32)
    middle = 1.5 * identity - 0.5 * iterate
    iterate = small_dot(middle, iterate, group)
    root = middle
    for step in range(1, NSIT):
        middle = 1.5 * identity - 0.5 * small_dot(iterate, root, group)
        if step < NSIT - 1:
            iterate = small_dot(middle, iterate, group)
        root = small_dot(root, middle, group)
    basis = jnp.sqrt(total_rows / scale) * small_dot(root, pz[0], group)
    own_lanes = basis
    for z in range(1, NZ):
        own_lanes = jnp.where(
            jnp.full((K, T), zh, jnp.int32) == z, pltpu.roll(basis, (NZ - z) * 32, 1), own_lanes
        )
    basis_ref[0] = own_lanes[:, :32]

    @pl.when(jnp.logical_not(at_last))
    def _():
        wait_for(rsem, CB, cb, n_in)
        wait_for(ssem, HZ, hz, 1)
        wait_for(ssem, JZ, jz, 1)

    @pl.when(at_last)
    def _():
        wait_for(rsem, CB, cb, n_in - 1)
        wait_for(ssem, GA, ga, NX * NY - 1)
        for _ in range(NZ - 1):
            wait_for(ssem, PZ, pz, 1)
        wait_for(ssem, CA, ca, NX * NY - 1)
        for at, buf in ((GB, gb), (CB, cb)):
            for _ in range(NZ - 1):
                wait_for(ssem, at, buf, n_in)
            wait_for(ssem, at, buf, n_in - 1)

    part = total_of(cb, n_in)
    for o in range(2):
        cross = from_flat([part[2 * o : 2 * o + 1], part[2 * o + 1 : 2 * o + 2]])
        elements = small_dot(root, cross, group) / jnp.sqrt(scale)
        elem_ref[0, o] = elements[:, :K]
    wait_for(ssem, VEC, vrecv, n_row - 1)
    wait_for(ssem, HY, hr, NY - 1)
    wait_for(ssem, JY, jr, NY - 1)


def solution(mesh):
    n_row, n_col = mesh.shape["row"], mesh.shape["col"]

    def per_device(vectors, h_tiles, h_list, j_tiles, j_list):
        hq, jq = h_tiles.shape[2], j_tiles.shape[2]
        total_rows = vectors.shape[2] * n_row * n_col
        hbm = pl.BlockSpec(memory_space=pltpu.HBM)
        vmem = pl.BlockSpec(memory_space=pltpu.VMEM)
        return pl.pallas_call(
            functools.partial(kernel, n_row, n_col, float(total_rows)),
            out_shape=(
                jax.ShapeDtypeStruct((1, K, 32), F32),
                jax.ShapeDtypeStruct((1, 2, K, K), F32),
            ),
            in_specs=[hbm] * 5,
            out_specs=(vmem, vmem),
            scratch_shapes=[
                pltpu.VMEM((1, K, 32), BF16),
                pltpu.VMEM((K, T), BF16),
                pltpu.VMEM((n_row, K, T), BF16),
                pltpu.VMEM((6, K, T), F32),
                pltpu.VMEM((hq, T, T), BF16),
                pltpu.VMEM((jq, T, T), BF16),
                pltpu.SMEM((1, 1, hq), jnp.int32),
                pltpu.SMEM((1, 1, jq), jnp.int32),
                pltpu.VMEM((NY, K, T), F32),
                pltpu.VMEM((NY, K, T), F32),
                pltpu.VMEM((NY, 2 * K, T), F32),
                pltpu.VMEM((NY, 2 * K, T), F32),
                pltpu.VMEM((NZ, K, T), F32),
                pltpu.VMEM((NZ, 2 * K, T), F32),
                pltpu.VMEM((1, K, T), F32),
                pltpu.VMEM((2, T), F32),
                pltpu.VMEM((NX * NY, 2, T), F32),
                pltpu.VMEM((n_row // NX, 2, T), F32),
                pltpu.VMEM((4, T), F32),
                pltpu.VMEM((NX * NY, 4, T), F32),
                pltpu.VMEM((n_row // NX, 4, T), F32),
                pltpu.SemaphoreType.DMA((5,)),
                pltpu.SemaphoreType.DMA((10,)),
                pltpu.SemaphoreType.DMA((10,)),
            ],
            compiler_params=pltpu.CompilerParams(
                collective_id=0, has_side_effects=True, vmem_limit_bytes=60 * 1024 * 1024
            ),
        )(
            vectors,
            h_tiles.reshape(hq, T, T),
            h_list,
            j_tiles.reshape(jq, T, T),
            j_list,
        )

    return jax.shard_map(
        per_device,
        mesh=mesh,
        in_specs=(
            P(None, None, ("col", "row")),
            P(None, "row", "col", None, None),
            P(None, "row", "col"),
            P(None, "row", "col", None, None),
            P(None, "row", "col"),
        ),
        out_specs=(P(None, None, ("row", "col")), P()),
        check_vma=False,
    )
```

```python
import functools

import jax
import jax.numpy as jnp
from jax import lax
from jax.experimental import pallas as pl
from jax.experimental.pallas import tpu as pltpu
from jax.sharding import PartitionSpec as P

NSIT = 6
MESH = pl.DeviceIdType.MESH
F32 = jnp.float32
BF16 = jnp.bfloat16
NY = 8
NZ = 4
NX = 4
VEC, HY, JY, HZ, JZ, PZ, GA, CA, GB, CB, HU, JU = range(12)
K = 16
T = 128
NT = (((1,), (1,)), ((), ()))


def iota(shape, dim):
    return lax.broadcasted_iota(jnp.int32, shape, dim)


def three_parts(x):
    a = x.astype(BF16).astype(F32)
    rest = x - a
    b = rest.astype(BF16).astype(F32)
    return a, b, rest - b


def small_dot(left, right, group):
    a1, a2, a3 = three_parts(left)
    b1, b2, b3 = (b.astype(BF16) for b in three_parts(right))
    lhs = jnp.where(
        (group == 0) | (group == 1) | (group == 4),
        a1,
        jnp.where((group == 5) | (group == 7), a3, a2),
    )
    rhs = jnp.concatenate([b1, b2, b1, b2, b3, b1, b3, b2], axis=0)
    return jnp.dot(lhs.astype(BF16), rhs, preferred_element_type=F32)


def long_dot(left, right):
    return lax.dot_general(
        left, right, NT, precision=lax.Precision.HIGHEST, preferred_element_type=F32
    )


def coded(piece, first):
    top = jnp.max(jnp.abs(piece), axis=1, keepdims=True)
    unit = (jnp.maximum(top, 1e-30) * (1.01 / 32767)).astype(BF16).astype(F32)
    steps = piece * jnp.broadcast_to(1.0 / unit, (K, T))
    steps = (steps + jnp.where(steps >= 0, 0.5, -0.5)).astype(jnp.int32).astype(jnp.int16)
    place = iota((K, T), 1) == iota((K, T), 0) + first
    units = jnp.sum(
        jnp.where(place, jnp.broadcast_to(unit, (K, T)), 0.0), axis=0, keepdims=True
    )
    return steps, units


def decoded_total(steps, units, rows):
    own = iota((rows, T), 1) == iota((rows, T), 0)
    spread = jnp.concatenate(
        [
            jnp.where(own, jnp.broadcast_to(units[d], (rows, T)), 0.0).astype(BF16)
            for d in range(NY)
        ],
        axis=0,
    )
    unit = jnp.dot(spread, jnp.ones((T, T), BF16), preferred_element_type=F32)
    parts = [
        steps[d].astype(jnp.int32).astype(F32) * unit[d * rows : (d + 1) * rows] for d in range(NY)
    ]
    while len(parts) > 1:
        parts = [parts[k] + parts[k + 1] for k in range(0, len(parts), 2)]
    return parts[0]


def flat_rows(repeated):
    own = iota((8, T), 1) // K == iota((8, T), 0)
    return [
        jnp.sum(jnp.where(own, repeated[8 * h : 8 * h + 8], 0.0), axis=0, keepdims=True)
        for h in range(2)
    ]


def from_flat(rows):
    own = iota((8, T), 1) // K == iota((8, T), 0)
    full = jnp.concatenate(
        [jnp.where(own, jnp.broadcast_to(row, (8, T)), 0.0) for row in rows], axis=0
    )
    for shift in (64, 32, 16):
        full = full + pltpu.roll(full, shift, 1)
    return full


def kernel(
    n_row, n_col, total_rows,
    vec_hbm, ht_hbm, hl_hbm, jt_hbm, jl_hbm, basis_ref, elem_ref,
    vloc, vsend, vrecv, vblk, ht, jt, hl, jl, hs, hr, js, jr, hsu, hru, jsu, jru, hz, jz, pz, gs, ga, gb, cs, ca, cb,
    lsem, ssem, rsem,
):
    me_r = lax.axis_index("row")
    me_c = lax.axis_index("col")
    zh = me_c // NY
    y = me_c % NY
    x = me_r // (n_row // NX)
    inner = me_r % (n_row // NX)
    n_in = n_row // NX
    last = NZ - 1
    at_last = zh == last
    barrier = pltpu.get_barrier_semaphore()

    def wrap(value, count):
        return jnp.where(value >= count, value - count, value)

    def at_row(d):
        return {"row": wrap(me_r + d, n_row)}

    def at_y(d):
        return {"col": zh * NY + wrap(y + d, NY)}

    def at_z(d):
        return {"col": wrap(zh + d, NZ) * NY + y}

    def at_plane(d):
        to = y * NX + x + d
        to = wrap(to, NX * NY)
        return {"row": (to % NX) * n_in + inner, "col": zh * NY + to // NX}

    def at_line(d):
        to = wrap(zh * n_in + inner + d, NZ * n_in)
        return {"row": x * n_in + to % n_in, "col": (to // n_in) * NY + y}

    def at_collector(d):
        return {"col": last * NY + y}

    codes = [
        pltpu.make_async_copy(hl_hbm, hl, lsem.at[3]),
        pltpu.make_async_copy(jl_hbm, jl, lsem.at[4]),
    ]
    loads = [
        pltpu.make_async_copy(vec_hbm, vloc, lsem.at[0]),
        pltpu.make_async_copy(ht_hbm, ht, lsem.at[1]),
        pltpu.make_async_copy(jt_hbm, jt, lsem.at[2]),
    ]

    def greet(where):
        def step(d, carry):
            pl.semaphore_signal(barrier, inc=1, device_id=where(d), device_id_type=MESH)
            return carry
        return step

    def send_all(at, where, count, src, dst):
        def step(d, carry):
            pltpu.make_async_remote_copy(
                src_ref=src(d), dst_ref=dst, send_sem=ssem.at[at], recv_sem=rsem.at[at],
                device_id=where(d), device_id_type=MESH,
            ).start()
            return carry
        lax.fori_loop(1, count + 1, step, 0)

    def wait_for(sem, at, buf, count):
        part = buf.at[pl.ds(0, count)]
        pltpu.make_async_copy(part, part, sem.at[at]).wait()

    def total_of(buf, count):
        parts = [buf[d] for d in range(count)]
        while len(parts) > 1:
            parts = [sum(parts[k + 1 : k + 2], parts[k]) for k in range(0, len(parts), 2)]
        return parts[0]

    lax.fori_loop(1, n_row, greet(at_row), 0)
    lax.fori_loop(1, NY, greet(at_y), 0)
    lax.fori_loop(1, NZ, greet(at_z), 0)
    for load in [loads[0]] + codes + loads[1:]:
        load.start()
    loads[0].wait()
    place = (iota((32, T), 1) == iota((32, T), 0) + 32 * lax.rem(me_r, 4)).astype(F32).astype(BF16)
    mine = jnp.dot(vloc[0], place, preferred_element_type=F32).astype(BF16)
    vsend[...] = mine
    vrecv[me_r] = mine
    for load in codes:
        load.wait()

    pl.semaphore_wait(barrier, n_row - 1 + NY - 1 + NZ - 1)
    send_all(VEC, at_row, n_row - 1, lambda d: vsend, vrecv.at[me_r])
    loads[1].wait()
    loads[2].wait()
    wait_for(rsem, VEC, vrecv, n_row - 1)

    for c in range(6):
        block = (vrecv[4 * c].astype(F32) + vrecv[4 * c + 1].astype(F32)) + (
            vrecv[4 * c + 2].astype(F32) + vrecv[4 * c + 3].astype(F32)
        )
        vblk[c] = block

    def masked(code, blocks):
        m = lax.shift_right_arithmetic(code * 43, 8)
        picked = vblk[code - 6 * m]
        which = jnp.full((K, T), m, jnp.int32)
        return jnp.concatenate(
            [jnp.where(which == b, picked, 0.0).astype(BF16) for b in range(blocks)], axis=0
        )

    def products(codes, tiles, count, blocks):
        total = jnp.zeros((blocks * K, T), F32)
        for q in range(0, count, 2):
            left = jnp.concatenate([masked(codes[0, 0, q + e], blocks) for e in range(2)], axis=1)
            right = jnp.concatenate([tiles[q + e] for e in range(2)], axis=1)
            total = total + lax.dot_general(left, right, NT, preferred_element_type=F32)
        return total

    lane32 = iota((K, T), 1) // 32

    def packed(total, first, yh, s):
        out = None
        for z in range(NZ):
            at = (first + 2 * z + yh) * K
            piece = total[at : at + K]
            shift = ((z - s) % NZ) * 32
            if shift:
                piece = pltpu.roll(piece, shift, 1)
            out = piece if out is None else jnp.where(lane32 == z, piece, out)
        return out

    h_total = products(hl, ht, ht.shape[0], 8)
    for yh in range(2):
        for s in range(4):
            hs[yh * 4 + s], hsu[yh * 4 + s] = coded(packed(h_total, 0, yh, s), 0)
    hr[y] = hs[y]
    hru[y] = hsu[y]
    send_all(HU, at_y, NY - 1, lambda d: hsu.at[wrap(y + d, NY)], hru.at[y])
    send_all(HY, at_y, NY - 1, lambda d: hs.at[wrap(y + d, NY)], hr.at[y])

    j_total = products(jl, jt, jt.shape[0], 16)
    for yh in range(2):
        for s in range(4):
            first, first_units = coded(packed(j_total, 0, yh, s), 0)
            second, second_units = coded(packed(j_total, 8, yh, s), K)
            js[yh * 4 + s, :K] = first
            js[yh * 4 + s, K:] = second
            jsu[yh * 4 + s] = first_units + second_units
    jr[y] = js[y]
    jru[y] = jsu[y]
    send_all(JU, at_y, NY - 1, lambda d: jsu.at[wrap(y + d, NY)], jru.at[y])
    send_all(JY, at_y, NY - 1, lambda d: js.at[wrap(y + d, NY)], jr.at[y])

    wait_for(rsem, HU, hru, NY - 1)
    wait_for(rsem, HY, hr, NY - 1)
    hz[zh] = decoded_total(hr, hru, K)

    @pl.when(jnp.logical_not(at_last))
    def _():
        send_all(HZ, at_collector, 1, lambda d: hz.at[zh], hz.at[zh])
        wait_for(rsem, JU, jru, NY - 1)
        wait_for(rsem, JY, jr, NY - 1)
        jz[zh] = decoded_total(jr, jru, 2 * K)
        send_all(JZ, at_collector, 1, lambda d: jz.at[zh], jz.at[zh])
        wait_for(rsem, PZ, pz, 1)

    @pl.when(at_last)
    def _():
        slot = y * NX + x
        wait_for(rsem, HZ, hz, NZ - 1)
        proj = total_of(hz, NZ)
        pz[0] = proj
        rows = flat_rows(long_dot(proj, jnp.concatenate([proj] * 8, axis=0)))
        for h in range(2):
            gs[h : h + 1] = rows[h]
            ga[slot, h : h + 1] = rows[h]
        send_all(GA, at_plane, NX * NY - 1, lambda d: gs, ga.at[slot])
        send_all(PZ, at_z, NZ - 1, lambda d: pz.at[0], pz.at[0])

        wait_for(rsem, JU, jru, NY - 1)
        wait_for(rsem, JY, jr, NY - 1)
        jz[zh] = decoded_total(jr, jru, 2 * K)
        wait_for(rsem, JZ, jz, NZ - 1)
        share = total_of(jz, NZ)
        for o in range(2):
            rows = flat_rows(
                long_dot(proj, jnp.concatenate([share[o * K : o * K + K]] * 8, axis=0))
            )
            for h in range(2):
                cs[2 * o + h : 2 * o + h + 1] = rows[h]
                ca[slot, 2 * o + h : 2 * o + h + 1] = rows[h]
        send_all(CA, at_plane, NX * NY - 1, lambda d: cs, ca.at[slot])

        wait_for(rsem, GA, ga, NX * NY - 1)
        gb[inner] = total_of(ga, NX * NY)
        send_all(GB, at_line, NZ * n_in - 1, lambda d: gb.at[inner], gb.at[inner])
        wait_for(rsem, CA, ca, NX * NY - 1)
        cb[inner] = total_of(ca, NX * NY)
        send_all(CB, at_line, NZ * n_in - 1, lambda d: cb.at[inner], cb.at[inner])
        wait_for(rsem, GB, gb, n_in - 1)

    @pl.when(jnp.logical_not(at_last))
    def _():
        wait_for(rsem, GB, gb, n_in)

    part = total_of(gb, n_in)
    square = jnp.sum(jnp.sum(part * part, axis=1, keepdims=True), axis=0, keepdims=True)
    scale = jnp.sqrt(jnp.broadcast_to(square, (K, T)) + 1e-06)
    iterate = from_flat([part[0:1], part[1:2]]) / scale
    group = iota((K, T), 1) // K
    identity = (iota((K, T), 1) % K == iota((K, T), 0)).astype(F32)
    middle = 1.5 * identity - 0.5 * iterate
    iterate = small_dot(middle, iterate, group)
    root = middle
    for step in range(1, NSIT):
        middle = 1.5 * identity - 0.5 * small_dot(iterate, root, group)
        if step < NSIT - 1:
            iterate = small_dot(middle, iterate, group)
        root = small_dot(root, middle, group)
    basis = jnp.sqrt(total_rows / scale) * small_dot(root, pz[0], group)
    own_lanes = basis
    for z in range(1, NZ):
        own_lanes = jnp.where(
            jnp.full((K, T), zh, jnp.int32) == z, pltpu.roll(basis, (NZ - z) * 32, 1), own_lanes
        )
    basis_ref[0] = own_lanes[:, :32]

    @pl.when(jnp.logical_not(at_last))
    def _():
        wait_for(rsem, CB, cb, n_in)
        wait_for(ssem, HZ, hz, 1)
        wait_for(ssem, JZ, jz, 1)

    @pl.when(at_last)
    def _():
        wait_for(rsem, CB, cb, n_in - 1)
        wait_for(ssem, GA, ga, NX * NY - 1)
        for _ in range(NZ - 1):
            wait_for(ssem, PZ, pz, 1)
        wait_for(ssem, CA, ca, NX * NY - 1)
        for at, buf in ((GB, gb), (CB, cb)):
            for _ in range(NZ - 1):
                wait_for(ssem, at, buf, n_in)
            wait_for(ssem, at, buf, n_in - 1)

    part = total_of(cb, n_in)
    for o in range(2):
        cross = from_flat([part[2 * o : 2 * o + 1], part[2 * o + 1 : 2 * o + 2]])
        elements = small_dot(root, cross, group) / jnp.sqrt(scale)
        elem_ref[0, o] = elements[:, :K]
    wait_for(ssem, VEC, vrecv, n_row - 1)
    wait_for(ssem, HY, hr, NY - 1)
    wait_for(ssem, JY, jr, NY - 1)
    wait_for(ssem, HU, hru, NY - 1)
    wait_for(ssem, JU, jru, NY - 1)


def solution(mesh):
    n_row, n_col = mesh.shape["row"], mesh.shape["col"]

    def per_device(vectors, h_tiles, h_list, j_tiles, j_list):
        hq, jq = h_tiles.shape[2], j_tiles.shape[2]
        total_rows = vectors.shape[2] * n_row * n_col
        hbm = pl.BlockSpec(memory_space=pltpu.HBM)
        vmem = pl.BlockSpec(memory_space=pltpu.VMEM)
        return pl.pallas_call(
            functools.partial(kernel, n_row, n_col, float(total_rows)),
            out_shape=(
                jax.ShapeDtypeStruct((1, K, 32), F32),
                jax.ShapeDtypeStruct((1, 2, K, K), F32),
            ),
            in_specs=[hbm] * 5,
            out_specs=(vmem, vmem),
            scratch_shapes=[
                pltpu.VMEM((1, K, 32), BF16),
                pltpu.VMEM((K, T), BF16),
                pltpu.VMEM((n_row, K, T), BF16),
                pltpu.VMEM((6, K, T), F32),
                pltpu.VMEM((hq, T, T), BF16),
                pltpu.VMEM((jq, T, T), BF16),
                pltpu.SMEM((1, 1, hq), jnp.int32),
                pltpu.SMEM((1, 1, jq), jnp.int32),
                pltpu.VMEM((NY, K, T), jnp.int16),
                pltpu.VMEM((NY, K, T), jnp.int16),
                pltpu.VMEM((NY, 2 * K, T), jnp.int16),
                pltpu.VMEM((NY, 2 * K, T), jnp.int16),
                pltpu.VMEM((NY, 1, T), F32),
                pltpu.VMEM((NY, 1, T), F32),
                pltpu.VMEM((NY, 1, T), F32),
                pltpu.VMEM((NY, 1, T), F32),
                pltpu.VMEM((NZ, K, T), F32),
                pltpu.VMEM((NZ, 2 * K, T), F32),
                pltpu.VMEM((1, K, T), F32),
                pltpu.VMEM((2, T), F32),
                pltpu.VMEM((NX * NY, 2, T), F32),
                pltpu.VMEM((n_row // NX, 2, T), F32),
                pltpu.VMEM((4, T), F32),
                pltpu.VMEM((NX * NY, 4, T), F32),
                pltpu.VMEM((n_row // NX, 4, T), F32),
                pltpu.SemaphoreType.DMA((5,)),
                pltpu.SemaphoreType.DMA((12,)),
                pltpu.SemaphoreType.DMA((12,)),
            ],
            compiler_params=pltpu.CompilerParams(
                collective_id=0, has_side_effects=True, vmem_limit_bytes=60 * 1024 * 1024
            ),
        )(
            vectors,
            h_tiles.reshape(hq, T, T),
            h_list,
            j_tiles.reshape(jq, T, T),
            j_list,
        )

    return jax.shard_map(
        per_device,
        mesh=mesh,
        in_specs=(
            P(None, None, ("col", "row")),
            P(None, "row", "col", None, None),
            P(None, "row", "col"),
            P(None, "row", "col", None, None),
            P(None, "row", "col"),
        ),
        out_specs=(P(None, None, ("row", "col")), P()),
        check_vma=False,
    )
```

```python
import functools

import jax
import jax.numpy as jnp
from jax import lax
from jax.experimental import pallas as pl
from jax.experimental.pallas import tpu as pltpu
from jax.sharding import PartitionSpec as P

NSIT = 6
MESH = pl.DeviceIdType.MESH
F32 = jnp.float32
BF16 = jnp.bfloat16
NY = 8
NZ = 4
NX = 4
VEC, HY, JY, HZ, JZ, PZ, GA, CA, GB, CB, HU, JU = range(12)
K = 16
T = 128
NT = (((1,), (1,)), ((), ()))


def iota(shape, dim):
    return lax.broadcasted_iota(jnp.int32, shape, dim)


def three_parts(x):
    a = x.astype(BF16).astype(F32)
    rest = x - a
    b = rest.astype(BF16).astype(F32)
    return a, b, rest - b


def small_dot(left, right, group):
    a1, a2, a3 = three_parts(left)
    b1, b2, b3 = (b.astype(BF16) for b in three_parts(right))
    lhs = jnp.where(
        (group == 0) | (group == 1) | (group == 4),
        a1,
        jnp.where((group == 5) | (group == 7), a3, a2),
    )
    rhs = jnp.concatenate([b1, b2, b1, b2, b3, b1, b3, b2], axis=0)
    return jnp.dot(lhs.astype(BF16), rhs, preferred_element_type=F32)


def long_dot(left, right):
    return lax.dot_general(
        left, right, NT, precision=lax.Precision.HIGHEST, preferred_element_type=F32
    )


def coded(piece, first):
    top = jnp.max(jnp.abs(piece), axis=1, keepdims=True)
    unit = (jnp.maximum(top, 1e-30) * (1.01 / 32767)).astype(BF16).astype(F32)
    steps = piece * jnp.broadcast_to(1.0 / unit, (K, T))
    steps = (steps + jnp.where(steps >= 0, 0.5, -0.5)).astype(jnp.int32).astype(jnp.int16)
    place = iota((K, T), 1) == iota((K, T), 0) + first
    units = jnp.sum(
        jnp.where(place, jnp.broadcast_to(unit, (K, T)), 0.0), axis=0, keepdims=True
    )
    return steps, units


def decoded_total(steps, units, rows):
    own = iota((rows, T), 1) == iota((rows, T), 0)
    spread = jnp.concatenate(
        [
            jnp.where(own, jnp.broadcast_to(units[d], (rows, T)), 0.0).astype(BF16)
            for d in range(NY)
        ],
        axis=0,
    )
    unit = jnp.dot(spread, jnp.ones((T, T), BF16), preferred_element_type=F32)
    parts = [
        steps[d].astype(jnp.int32).astype(F32) * unit[d * rows : (d + 1) * rows] for d in range(NY)
    ]
    while len(parts) > 1:
        parts = [parts[k] + parts[k + 1] for k in range(0, len(parts), 2)]
    return parts[0]


def flat_rows(repeated):
    own = iota((8, T), 1) // K == iota((8, T), 0)
    return [
        jnp.sum(jnp.where(own, repeated[8 * h : 8 * h + 8], 0.0), axis=0, keepdims=True)
        for h in range(2)
    ]


def from_flat(rows):
    own = iota((8, T), 1) // K == iota((8, T), 0)
    full = jnp.concatenate(
        [jnp.where(own, jnp.broadcast_to(row, (8, T)), 0.0) for row in rows], axis=0
    )
    for shift in (64, 32, 16):
        full = full + pltpu.roll(full, shift, 1)
    return full


def kernel(
    n_row, n_col, total_rows,
    vec_hbm, ht_hbm, hl_hbm, jt_hbm, jl_hbm, basis_ref, elem_ref,
    vloc, vsend, vrecv, vblk, ht, jt, hl, jl, hs, hr, js, jr, hsu, hru, jsu, jru, hz, jz, pz, gs, ga, gb, cs, ca, cb,
    lsem, ssem, rsem,
):
    me_r = lax.axis_index("row")
    me_c = lax.axis_index("col")
    zh = me_c // NY
    y = me_c % NY
    x = me_r // (n_row // NX)
    inner = me_r % (n_row // NX)
    n_in = n_row // NX
    last = NZ - 1
    at_last = zh == last
    barrier = pltpu.get_barrier_semaphore()

    def wrap(value, count):
        return jnp.where(value >= count, value - count, value)

    def at_row(d):
        return {"row": wrap(me_r + d, n_row)}

    def at_y(d):
        return {"col": zh * NY + wrap(y + d, NY)}

    def at_z(d):
        return {"col": wrap(zh + d, NZ) * NY + y}

    def at_plane(d):
        to = y * NX + x + d
        to = wrap(to, NX * NY)
        return {"row": (to % NX) * n_in + inner, "col": zh * NY + to // NX}

    def at_line(d):
        to = wrap(zh * n_in + inner + d, NZ * n_in)
        return {"row": x * n_in + to % n_in, "col": (to // n_in) * NY + y}

    def at_collector(d):
        return {"col": last * NY + y}

    codes = [
        pltpu.make_async_copy(hl_hbm, hl, lsem.at[3]),
        pltpu.make_async_copy(jl_hbm, jl, lsem.at[4]),
    ]
    loads = [
        pltpu.make_async_copy(vec_hbm, vloc, lsem.at[0]),
        pltpu.make_async_copy(ht_hbm, ht, lsem.at[1]),
        pltpu.make_async_copy(jt_hbm, jt, lsem.at[2]),
    ]

    def greet(where):
        def step(d, carry):
            pl.semaphore_signal(barrier, inc=1, device_id=where(d), device_id_type=MESH)
            return carry
        return step

    def send_all(at, where, count, src, dst):
        def step(d, carry):
            pltpu.make_async_remote_copy(
                src_ref=src(d), dst_ref=dst, send_sem=ssem.at[at], recv_sem=rsem.at[at],
                device_id=where(d), device_id_type=MESH,
            ).start()
            return carry
        lax.fori_loop(1, count + 1, step, 0)

    def wait_for(sem, at, buf, count):
        part = buf.at[pl.ds(0, count)]
        pltpu.make_async_copy(part, part, sem.at[at]).wait()

    def total_of(buf, count):
        parts = [buf[d] for d in range(count)]
        while len(parts) > 1:
            parts = [sum(parts[k + 1 : k + 2], parts[k]) for k in range(0, len(parts), 2)]
        return parts[0]

    lax.fori_loop(1, n_row, greet(at_row), 0)
    lax.fori_loop(1, NY, greet(at_y), 0)
    lax.fori_loop(1, NZ, greet(at_z), 0)
    for load in [loads[0]] + codes + loads[1:]:
        load.start()
    loads[0].wait()
    place = (iota((32, T), 1) == iota((32, T), 0) + 32 * lax.rem(me_r, 4)).astype(F32).astype(BF16)
    mine = jnp.dot(vloc[0], place, preferred_element_type=F32).astype(BF16)
    vsend[...] = mine
    vrecv[me_r] = mine
    for load in codes:
        load.wait()

    pl.semaphore_wait(barrier, n_row - 1 + NY - 1 + NZ - 1)
    send_all(VEC, at_row, n_row - 1, lambda d: vsend, vrecv.at[me_r])
    loads[1].wait()
    loads[2].wait()
    wait_for(rsem, VEC, vrecv, n_row - 1)

    for c in range(6):
        block = (vrecv[4 * c].astype(F32) + vrecv[4 * c + 1].astype(F32)) + (
            vrecv[4 * c + 2].astype(F32) + vrecv[4 * c + 3].astype(F32)
        )
        vblk[c] = block

    def masked(code, blocks):
        m = lax.shift_right_arithmetic(code * 43, 8)
        picked = vblk[code - 6 * m]
        which = jnp.full((K, T), m, jnp.int32)
        return jnp.concatenate(
            [jnp.where(which == b, picked, 0.0).astype(BF16) for b in range(blocks)], axis=0
        )

    def products(codes, tiles, count, blocks):
        total = jnp.zeros((blocks * K, T), F32)
        for q in range(0, count, 2):
            left = jnp.concatenate([masked(codes[0, 0, q + e], blocks) for e in range(2)], axis=1)
            right = jnp.concatenate([tiles[q + e] for e in range(2)], axis=1)
            total = total + lax.dot_general(left, right, NT, preferred_element_type=F32)
        return total

    lane32 = iota((K, T), 1) // 32

    def packed(total, first, yh, s):
        out = None
        for z in range(NZ):
            at = (first + 2 * z + yh) * K
            piece = total[at : at + K]
            shift = ((z - s) % NZ) * 32
            if shift:
                piece = pltpu.roll(piece, shift, 1)
            out = piece if out is None else jnp.where(lane32 == z, piece, out)
        return out

    h_total = products(hl, ht, ht.shape[0], 8)
    for yh in range(2):
        for s in range(4):
            hs[yh * 4 + s], hsu[yh * 4 + s] = coded(packed(h_total, 0, yh, s), 0)
    hr[y] = hs[y]
    hru[y] = hsu[y]
    send_all(HU, at_y, NY - 1, lambda d: hsu.at[wrap(y + d, NY)], hru.at[y])
    send_all(HY, at_y, NY - 1, lambda d: hs.at[wrap(y + d, NY)], hr.at[y])

    j_total = products(jl, jt, jt.shape[0], 16)
    for yh in range(2):
        for s in range(4):
            first, first_units = coded(packed(j_total, 0, yh, s), 0)
            second, second_units = coded(packed(j_total, 8, yh, s), K)
            js[yh * 4 + s, :K] = first
            js[yh * 4 + s, K:] = second
            jsu[yh * 4 + s] = first_units + second_units
    jr[y] = js[y]
    jru[y] = jsu[y]
    send_all(JU, at_y, NY - 1, lambda d: jsu.at[wrap(y + d, NY)], jru.at[y])
    send_all(JY, at_y, NY - 1, lambda d: js.at[wrap(y + d, NY)], jr.at[y])

    wait_for(rsem, HU, hru, NY - 1)
    wait_for(rsem, HY, hr, NY - 1)
    hz[zh] = decoded_total(hr, hru, K)

    @pl.when(jnp.logical_not(at_last))
    def _():
        send_all(HZ, at_collector, 1, lambda d: hz.at[zh], hz.at[zh])
        wait_for(rsem, JU, jru, NY - 1)
        wait_for(rsem, JY, jr, NY - 1)
        jz[zh] = decoded_total(jr, jru, 2 * K)
        send_all(JZ, at_collector, 1, lambda d: jz.at[zh], jz.at[zh])
        wait_for(rsem, PZ, pz, 1)

    @pl.when(at_last)
    def _():
        slot = y * NX + x
        wait_for(rsem, HZ, hz, NZ - 1)
        proj = total_of(hz, NZ)
        pz[0] = proj
        rows = flat_rows(long_dot(proj, jnp.concatenate([proj] * 8, axis=0)))
        for h in range(2):
            gs[h : h + 1] = rows[h]
            ga[slot, h : h + 1] = rows[h]
        send_all(GA, at_plane, NX * NY - 1, lambda d: gs, ga.at[slot])
        send_all(PZ, at_z, NZ - 1, lambda d: pz.at[0], pz.at[0])

        wait_for(rsem, JU, jru, NY - 1)
        wait_for(rsem, JY, jr, NY - 1)
        jz[zh] = decoded_total(jr, jru, 2 * K)
        wait_for(rsem, JZ, jz, NZ - 1)
        share = total_of(jz, NZ)
        for o in range(2):
            rows = flat_rows(
                long_dot(proj, jnp.concatenate([share[o * K : o * K + K]] * 8, axis=0))
            )
            for h in range(2):
                cs[2 * o + h : 2 * o + h + 1] = rows[h]
                ca[slot, 2 * o + h : 2 * o + h + 1] = rows[h]
        send_all(CA, at_plane, NX * NY - 1, lambda d: cs, ca.at[slot])

        wait_for(rsem, GA, ga, NX * NY - 1)
        gb[inner] = total_of(ga, NX * NY)
        send_all(GB, at_line, NZ * n_in - 1, lambda d: gb.at[inner], gb.at[inner])
        wait_for(rsem, CA, ca, NX * NY - 1)
        cb[inner] = total_of(ca, NX * NY)
        send_all(CB, at_line, NZ * n_in - 1, lambda d: cb.at[inner], cb.at[inner])
        wait_for(rsem, GB, gb, n_in - 1)

    @pl.when(jnp.logical_not(at_last))
    def _():
        wait_for(rsem, GB, gb, n_in)

    part = total_of(gb, n_in)
    square = jnp.sum(jnp.sum(part * part, axis=1, keepdims=True), axis=0, keepdims=True)
    scale = jnp.sqrt(jnp.broadcast_to(square, (K, T)) + 1e-06)
    iterate = from_flat([part[0:1], part[1:2]]) / scale
    group = iota((K, T), 1) // K
    identity = (iota((K, T), 1) % K == iota((K, T), 0)).astype(F32)
    middle = 1.5 * identity - 0.5 * iterate
    iterate = small_dot(middle, iterate, group)
    root = middle
    for step in range(1, NSIT):
        middle = 1.5 * identity - 0.5 * small_dot(iterate, root, group)
        if step < NSIT - 1:
            iterate = small_dot(middle, iterate, group)
        root = small_dot(root, middle, group)
    basis = jnp.sqrt(total_rows / scale) * small_dot(root, pz[0], group)
    own_lanes = basis
    for z in range(1, NZ):
        own_lanes = jnp.where(
            jnp.full((K, T), zh, jnp.int32) == z, pltpu.roll(basis, (NZ - z) * 32, 1), own_lanes
        )
    basis_ref[0] = own_lanes[:, :32]

    scaled = root / jnp.sqrt(scale)

    @pl.when(jnp.logical_not(at_last))
    def _():
        wait_for(rsem, CB, cb, n_in)

    @pl.when(at_last)
    def _():
        wait_for(rsem, CB, cb, n_in - 1)

    part = total_of(cb, n_in)
    for o in range(2):
        cross = from_flat([part[2 * o : 2 * o + 1], part[2 * o + 1 : 2 * o + 2]])
        elem_ref[0, o] = small_dot(scaled, cross, group)[:, :K]

    @pl.when(jnp.logical_not(at_last))
    def _():
        wait_for(ssem, HZ, hz, 1)
        wait_for(ssem, JZ, jz, 1)

    @pl.when(at_last)
    def _():
        wait_for(ssem, GA, ga, NX * NY - 1)
        for _ in range(NZ - 1):
            wait_for(ssem, PZ, pz, 1)
        wait_for(ssem, CA, ca, NX * NY - 1)
        for at, buf in ((GB, gb), (CB, cb)):
            for _ in range(NZ - 1):
                wait_for(ssem, at, buf, n_in)
            wait_for(ssem, at, buf, n_in - 1)

    wait_for(ssem, VEC, vrecv, n_row - 1)
    wait_for(ssem, HY, hr, NY - 1)
    wait_for(ssem, JY, jr, NY - 1)
    wait_for(ssem, HU, hru, NY - 1)
    wait_for(ssem, JU, jru, NY - 1)


def solution(mesh):
    n_row, n_col = mesh.shape["row"], mesh.shape["col"]

    def per_device(vectors, h_tiles, h_list, j_tiles, j_list):
        hq, jq = h_tiles.shape[2], j_tiles.shape[2]
        total_rows = vectors.shape[2] * n_row * n_col
        hbm = pl.BlockSpec(memory_space=pltpu.HBM)
        vmem = pl.BlockSpec(memory_space=pltpu.VMEM)
        return pl.pallas_call(
            functools.partial(kernel, n_row, n_col, float(total_rows)),
            out_shape=(
                pltpu.VMEM((1, K, 32), F32),
                pltpu.VMEM((1, 2, K, K), F32),
            ),
            in_specs=[hbm] * 5,
            out_specs=(vmem, vmem),
            scratch_shapes=[
                pltpu.VMEM((1, K, 32), BF16),
                pltpu.VMEM((K, T), BF16),
                pltpu.VMEM((n_row, K, T), BF16),
                pltpu.VMEM((6, K, T), F32),
                pltpu.VMEM((hq, T, T), BF16),
                pltpu.VMEM((jq, T, T), BF16),
                pltpu.SMEM((1, 1, hq), jnp.int32),
                pltpu.SMEM((1, 1, jq), jnp.int32),
                pltpu.VMEM((NY, K, T), jnp.int16),
                pltpu.VMEM((NY, K, T), jnp.int16),
                pltpu.VMEM((NY, 2 * K, T), jnp.int16),
                pltpu.VMEM((NY, 2 * K, T), jnp.int16),
                pltpu.VMEM((NY, 1, T), F32),
                pltpu.VMEM((NY, 1, T), F32),
                pltpu.VMEM((NY, 1, T), F32),
                pltpu.VMEM((NY, 1, T), F32),
                pltpu.VMEM((NZ, K, T), F32),
                pltpu.VMEM((NZ, 2 * K, T), F32),
                pltpu.VMEM((1, K, T), F32),
                pltpu.VMEM((2, T), F32),
                pltpu.VMEM((NX * NY, 2, T), F32),
                pltpu.VMEM((n_row // NX, 2, T), F32),
                pltpu.VMEM((4, T), F32),
                pltpu.VMEM((NX * NY, 4, T), F32),
                pltpu.VMEM((n_row // NX, 4, T), F32),
                pltpu.SemaphoreType.DMA((5,)),
                pltpu.SemaphoreType.DMA((12,)),
                pltpu.SemaphoreType.DMA((12,)),
            ],
            compiler_params=pltpu.CompilerParams(
                collective_id=0, has_side_effects=True, vmem_limit_bytes=60 * 1024 * 1024
            ),
        )(
            vectors,
            h_tiles.reshape(hq, T, T),
            h_list,
            j_tiles.reshape(jq, T, T),
            j_list,
        )

    return jax.shard_map(
        per_device,
        mesh=mesh,
        in_specs=(
            P(None, None, ("col", "row")),
            P(None, "row", "col", None, None),
            P(None, "row", "col"),
            P(None, "row", "col", None, None),
            P(None, "row", "col"),
        ),
        out_specs=(P(None, None, ("row", "col")), P()),
        check_vma=False,
    )
```

```python
import functools

import jax
import jax.numpy as jnp
from jax import lax
from jax.experimental import pallas as pl
from jax.experimental.pallas import tpu as pltpu
from jax.sharding import PartitionSpec as P

NSIT = 6
MESH = pl.DeviceIdType.MESH
F32 = jnp.float32
BF16 = jnp.bfloat16
NY = 8
NZ = 4
NX = 4
VEC, HY, JY, JZ, PZ, GA, CA, GB, CB, HU, JU = range(11)
K = 16
T = 128
NT = (((1,), (1,)), ((), ()))


def iota(shape, dim):
    return lax.broadcasted_iota(jnp.int32, shape, dim)


def three_parts(x):
    a = x.astype(BF16).astype(F32)
    rest = x - a
    b = rest.astype(BF16).astype(F32)
    return a, b, rest - b


def small_dot(left, right, group):
    a1, a2, a3 = three_parts(left)
    b1, b2, b3 = (b.astype(BF16) for b in three_parts(right))
    lhs = jnp.where(
        (group == 0) | (group == 1) | (group == 4),
        a1,
        jnp.where((group == 5) | (group == 7), a3, a2),
    )
    rhs = jnp.concatenate([b1, b2, b1, b2, b3, b1, b3, b2], axis=0)
    return jnp.dot(lhs.astype(BF16), rhs, preferred_element_type=F32)


def long_dot(left, right):
    return lax.dot_general(
        left, right, NT, precision=lax.Precision.HIGHEST, preferred_element_type=F32
    )


def coded(piece, first):
    top = jnp.max(jnp.abs(piece), axis=1, keepdims=True)
    unit = (jnp.maximum(top, 1e-30) * (1.01 / 32767)).astype(BF16).astype(F32)
    steps = piece * jnp.broadcast_to(1.0 / unit, (K, T))
    steps = (steps + jnp.where(steps >= 0, 0.5, -0.5)).astype(jnp.int32).astype(jnp.int16)
    place = iota((K, T), 1) == iota((K, T), 0) + first
    units = jnp.sum(
        jnp.where(place, jnp.broadcast_to(unit, (K, T)), 0.0), axis=0, keepdims=True
    )
    return steps, units


def spread_units(units, rows, count):
    own = iota((rows, T), 1) == iota((rows, T), 0)
    placed = jnp.concatenate(
        [
            jnp.where(own, jnp.broadcast_to(units[d], (rows, T)), 0.0).astype(BF16)
            for d in range(count)
        ],
        axis=0,
    )
    return jnp.dot(placed, jnp.ones((T, T), BF16), preferred_element_type=F32)


def decoded_total(steps, unit, rows, count):
    parts = [
        steps[d].astype(jnp.int32).astype(F32) * unit[d * rows : (d + 1) * rows]
        for d in range(count)
    ]
    while len(parts) > 1:
        parts = [parts[k] + parts[k + 1] for k in range(0, len(parts), 2)]
    return parts[0]


def flat_rows(repeated):
    own = iota((8, T), 1) // K == iota((8, T), 0)
    return [
        jnp.sum(jnp.where(own, repeated[8 * h : 8 * h + 8], 0.0), axis=0, keepdims=True)
        for h in range(2)
    ]


def from_flat(rows):
    own = iota((8, T), 1) // K == iota((8, T), 0)
    full = jnp.concatenate(
        [jnp.where(own, jnp.broadcast_to(row, (8, T)), 0.0) for row in rows], axis=0
    )
    for shift in (64, 32, 16):
        full = full + pltpu.roll(full, shift, 1)
    return full


def kernel(
    n_row, n_col, total_rows,
    vec_hbm, ht_hbm, hl_hbm, jt_hbm, jl_hbm, basis_ref, elem_ref,
    vloc, vsend, vrecv, vblk, ht, jt, hl, jl, hs, hr, js, jr, hsu, hru, jsu, jru, jz, pz, gs, ga, gb, cs, ca, cb,
    lsem, ssem, rsem, ready,
):
    me_r = lax.axis_index("row")
    me_c = lax.axis_index("col")
    zh = me_c // NY
    y = me_c % NY
    x = me_r // (n_row // NX)
    inner = me_r % (n_row // NX)
    n_in = n_row // NX
    last = NZ - 1
    at_last = zh == last
    barrier = pltpu.get_barrier_semaphore()

    def wrap(value, count):
        return jnp.where(value >= count, value - count, value)

    def at_row(d):
        return {"row": wrap(me_r + d, n_row)}

    def at_y(d):
        return {"col": zh * NY + wrap(y + d, NY)}

    def at_z(d):
        return {"col": wrap(zh + d, NZ) * NY + y}

    def at_plane(d):
        to = y * NX + x + d
        to = wrap(to, NX * NY)
        return {"row": (to % NX) * n_in + inner, "col": zh * NY + to // NX}

    def at_line(d):
        to = wrap(zh * n_in + inner + d, NZ * n_in)
        return {"row": x * n_in + to % n_in, "col": (to // n_in) * NY + y}

    def at_collector(d):
        return {"col": last * NY + wrap(y + d, NY)}

    codes = [
        pltpu.make_async_copy(hl_hbm, hl, lsem.at[3]),
        pltpu.make_async_copy(jl_hbm, jl, lsem.at[4]),
    ]
    loads = [
        pltpu.make_async_copy(vec_hbm, vloc, lsem.at[0]),
        pltpu.make_async_copy(ht_hbm, ht, lsem.at[1]),
        pltpu.make_async_copy(jt_hbm, jt, lsem.at[2]),
    ]

    def greet(where):
        def step(d, carry):
            pl.semaphore_signal(barrier, inc=1, device_id=where(d), device_id_type=MESH)
            return carry
        return step

    def send_all(at, where, count, src, dst):
        def step(d, carry):
            pltpu.make_async_remote_copy(
                src_ref=src(d), dst_ref=dst, send_sem=ssem.at[at], recv_sem=rsem.at[at],
                device_id=where(d), device_id_type=MESH,
            ).start()
            return carry
        lax.fori_loop(1, count + 1, step, 0)

    def wait_for(sem, at, buf, count):
        part = buf.at[pl.ds(0, count)]
        pltpu.make_async_copy(part, part, sem.at[at]).wait()

    def total_of(buf, count):
        parts = [buf[d] for d in range(count)]
        while len(parts) > 1:
            parts = [sum(parts[k + 1 : k + 2], parts[k]) for k in range(0, len(parts), 2)]
        return parts[0]

    lax.fori_loop(1, n_row, greet(at_row), 0)
    lax.fori_loop(1, NY, greet(at_y), 0)
    lax.fori_loop(1, NZ, greet(at_z), 0)
    for load in [loads[0]] + codes + loads[1:]:
        load.start()
    loads[0].wait()
    place = (iota((32, T), 1) == iota((32, T), 0) + 32 * lax.rem(me_r, 4)).astype(F32).astype(BF16)
    mine = jnp.dot(vloc[0], place, preferred_element_type=F32).astype(BF16)
    vsend[...] = mine
    vrecv[me_r] = mine
    for load in codes:
        load.wait()

    pl.semaphore_wait(barrier, n_row - 1 + NY - 1 + NZ - 1)
    @pl.when(at_last)
    def _():
        for d in range(1, NZ):
            pl.semaphore_signal(ready, inc=1, device_id=at_z(d), device_id_type=MESH)

    send_all(VEC, at_row, n_row - 1, lambda d: vsend, vrecv.at[me_r])
    loads[1].wait()
    loads[2].wait()
    wait_for(rsem, VEC, vrecv, n_row - 1)

    for c in range(6):
        block = (vrecv[4 * c].astype(F32) + vrecv[4 * c + 1].astype(F32)) + (
            vrecv[4 * c + 2].astype(F32) + vrecv[4 * c + 3].astype(F32)
        )
        vblk[c] = block

    def masked(code, blocks):
        m = lax.shift_right_arithmetic(code * 43, 8)
        picked = vblk[code - 6 * m]
        which = jnp.full((K, T), m, jnp.int32)
        return jnp.concatenate(
            [jnp.where(which == b, picked, 0.0).astype(BF16) for b in range(blocks)], axis=0
        )

    def products(codes, tiles, count, blocks):
        total = jnp.zeros((blocks * K, T), F32)
        for q in range(0, count, 2):
            left = jnp.concatenate([masked(codes[0, 0, q + e], blocks) for e in range(2)], axis=1)
            right = jnp.concatenate([tiles[q + e] for e in range(2)], axis=1)
            total = total + lax.dot_general(left, right, NT, preferred_element_type=F32)
        return total

    lane32 = iota((K, T), 1) // 32

    def packed(total, first, yh, s):
        out = None
        for z in range(NZ):
            at = (first + 2 * z + yh) * K
            piece = total[at : at + K]
            shift = ((z - s) % NZ) * 32
            if shift:
                piece = pltpu.roll(piece, shift, 1)
            out = piece if out is None else jnp.where(lane32 == z, piece, out)
        return out

    j_total = products(jl, jt, jt.shape[0], 16)
    for yh in range(2):
        for s in range(4):
            first, first_units = coded(packed(j_total, 0, yh, s), 0)
            second, second_units = coded(packed(j_total, 8, yh, s), K)
            js[yh * 4 + s, :K] = first
            js[yh * 4 + s, K:] = second
            jsu[yh * 4 + s] = first_units + second_units
    jr[y] = js[y]
    jru[y] = jsu[y]
    send_all(JU, at_y, NY - 1, lambda d: jsu.at[wrap(y + d, NY)], jru.at[y])
    send_all(JY, at_y, NY - 1, lambda d: js.at[wrap(y + d, NY)], jr.at[y])
    h_total = products(hl, ht, ht.shape[0], 8)
    for yh in range(2):
        for s in range(4):
            hs[yh * 4 + s], hsu[yh * 4 + s] = coded(packed(h_total, 0, yh, s), 0)

    def decode_j():
        wait_for(rsem, JU, jru, NY - 1)
        unit = spread_units(jru, 2 * K, NY)
        wait_for(rsem, JY, jr, NY - 1)
        jz[zh] = decoded_total(jr, unit, 2 * K, NY)

    @pl.when(jnp.logical_not(at_last))
    def _():
        pl.semaphore_wait(ready, 1)
        send_all(
            HU, lambda d: at_collector(d - 1), NY, lambda d: hsu.at[wrap(y + d - 1, NY)], hru.at[me_c]
        )
        send_all(
            HY, lambda d: at_collector(d - 1), NY, lambda d: hs.at[wrap(y + d - 1, NY)], hr.at[me_c]
        )
        decode_j()
        send_all(JZ, lambda d: at_collector(0), 1, lambda d: jz.at[zh], jz.at[zh])
        wait_for(rsem, PZ, pz, 1)
        wait_for(rsem, GB, gb, n_in)

    @pl.when(at_last)
    def _():
        slot = y * NX + x
        hr[me_c] = hs[y]
        hru[me_c] = hsu[y]
        send_all(HU, at_collector, NY - 1, lambda d: hsu.at[wrap(y + d, NY)], hru.at[me_c])
        send_all(HY, at_collector, NY - 1, lambda d: hs.at[wrap(y + d, NY)], hr.at[me_c])
        decode_j()
        wait_for(rsem, HU, hru, n_col - 1)
        unit = spread_units(hru, K, n_col)
        wait_for(rsem, HY, hr, n_col - 1)
        proj = decoded_total(hr, unit, K, n_col)
        pz[0] = proj
        rows = flat_rows(long_dot(proj, jnp.concatenate([proj] * 8, axis=0)))
        for h in range(2):
            gs[h : h + 1] = rows[h]
            ga[slot, h : h + 1] = rows[h]
        send_all(GA, at_plane, NX * NY - 1, lambda d: gs, ga.at[slot])
        send_all(PZ, at_z, NZ - 1, lambda d: pz.at[0], pz.at[0])

        wait_for(rsem, JZ, jz, NZ - 1)
        share = total_of(jz, NZ)
        for o in range(2):
            rows = flat_rows(
                long_dot(proj, jnp.concatenate([share[o * K : o * K + K]] * 8, axis=0))
            )
            for h in range(2):
                cs[2 * o + h : 2 * o + h + 1] = rows[h]
                ca[slot, 2 * o + h : 2 * o + h + 1] = rows[h]
        send_all(CA, at_plane, NX * NY - 1, lambda d: cs, ca.at[slot])

        wait_for(rsem, GA, ga, NX * NY - 1)
        gb[inner] = total_of(ga, NX * NY)
        send_all(GB, at_line, NZ * n_in - 1, lambda d: gb.at[inner], gb.at[inner])
        wait_for(rsem, CA, ca, NX * NY - 1)
        cb[inner] = total_of(ca, NX * NY)
        send_all(CB, at_line, NZ * n_in - 1, lambda d: cb.at[inner], cb.at[inner])
        wait_for(rsem, GB, gb, n_in - 1)

    part = total_of(gb, n_in)
    square = jnp.sum(jnp.sum(part * part, axis=1, keepdims=True), axis=0, keepdims=True)
    scale = jnp.sqrt(jnp.broadcast_to(square, (K, T)) + 1e-06)
    iterate = from_flat([part[0:1], part[1:2]]) / scale
    group = iota((K, T), 1) // K
    identity = (iota((K, T), 1) % K == iota((K, T), 0)).astype(F32)
    middle = 1.5 * identity - 0.5 * iterate
    iterate = small_dot(middle, iterate, group)
    root = middle
    for step in range(1, NSIT):
        middle = 1.5 * identity - 0.5 * small_dot(iterate, root, group)
        if step < NSIT - 1:
            iterate = small_dot(middle, iterate, group)
        root = small_dot(root, middle, group)
    basis = jnp.sqrt(total_rows / scale) * small_dot(root, pz[0], group)
    own_lanes = basis
    for z in range(1, NZ):
        own_lanes = jnp.where(
            jnp.full((K, T), zh, jnp.int32) == z, pltpu.roll(basis, (NZ - z) * 32, 1), own_lanes
        )
    basis_ref[0] = own_lanes[:, :32]

    scaled = root / jnp.sqrt(scale)

    @pl.when(jnp.logical_not(at_last))
    def _():
        wait_for(rsem, CB, cb, n_in)

    @pl.when(at_last)
    def _():
        wait_for(rsem, CB, cb, n_in - 1)

    part = total_of(cb, n_in)
    for o in range(2):
        cross = from_flat([part[2 * o : 2 * o + 1], part[2 * o + 1 : 2 * o + 2]])
        elem_ref[0, o] = small_dot(scaled, cross, group)[:, :K]

    @pl.when(jnp.logical_not(at_last))
    def _():
        wait_for(ssem, HU, hru, NY)
        wait_for(ssem, HY, hr, NY)
        wait_for(ssem, JZ, jz, 1)

    @pl.when(at_last)
    def _():
        wait_for(ssem, HU, hru, NY - 1)
        wait_for(ssem, HY, hr, NY - 1)
        wait_for(ssem, GA, ga, NX * NY - 1)
        for _ in range(NZ - 1):
            wait_for(ssem, PZ, pz, 1)
        wait_for(ssem, CA, ca, NX * NY - 1)
        for at, buf in ((GB, gb), (CB, cb)):
            for _ in range(NZ - 1):
                wait_for(ssem, at, buf, n_in)
            wait_for(ssem, at, buf, n_in - 1)

    wait_for(ssem, VEC, vrecv, n_row - 1)
    wait_for(ssem, JU, jru, NY - 1)
    wait_for(ssem, JY, jr, NY - 1)


def solution(mesh):
    n_row, n_col = mesh.shape["row"], mesh.shape["col"]

    def per_device(vectors, h_tiles, h_list, j_tiles, j_list):
        hq, jq = h_tiles.shape[2], j_tiles.shape[2]
        total_rows = vectors.shape[2] * n_row * n_col
        hbm = pl.BlockSpec(memory_space=pltpu.HBM)
        vmem = pl.BlockSpec(memory_space=pltpu.VMEM)
        return pl.pallas_call(
            functools.partial(kernel, n_row, n_col, float(total_rows)),
            out_shape=(
                pltpu.VMEM((1, K, 32), F32),
                pltpu.VMEM((1, 2, K, K), F32),
            ),
            in_specs=[hbm] * 5,
            out_specs=(vmem, vmem),
            scratch_shapes=[
                pltpu.VMEM((1, K, 32), BF16),
                pltpu.VMEM((K, T), BF16),
                pltpu.VMEM((n_row, K, T), BF16),
                pltpu.VMEM((6, K, T), F32),
                pltpu.VMEM((hq, T, T), BF16),
                pltpu.VMEM((jq, T, T), BF16),
                pltpu.SMEM((1, 1, hq), jnp.int32),
                pltpu.SMEM((1, 1, jq), jnp.int32),
                pltpu.VMEM((NY, K, T), jnp.int16),
                pltpu.VMEM((n_col, K, T), jnp.int16),
                pltpu.VMEM((NY, 2 * K, T), jnp.int16),
                pltpu.VMEM((NY, 2 * K, T), jnp.int16),
                pltpu.VMEM((NY, 1, T), F32),
                pltpu.VMEM((n_col, 1, T), F32),
                pltpu.VMEM((NY, 1, T), F32),
                pltpu.VMEM((NY, 1, T), F32),
                pltpu.VMEM((NZ, 2 * K, T), F32),
                pltpu.VMEM((1, K, T), F32),
                pltpu.VMEM((2, T), F32),
                pltpu.VMEM((NX * NY, 2, T), F32),
                pltpu.VMEM((n_row // NX, 2, T), F32),
                pltpu.VMEM((4, T), F32),
                pltpu.VMEM((NX * NY, 4, T), F32),
                pltpu.VMEM((n_row // NX, 4, T), F32),
                pltpu.SemaphoreType.DMA((5,)),
                pltpu.SemaphoreType.DMA((12,)),
                pltpu.SemaphoreType.DMA((12,)),
                pltpu.SemaphoreType.REGULAR,
            ],
            compiler_params=pltpu.CompilerParams(
                collective_id=0, has_side_effects=True, vmem_limit_bytes=60 * 1024 * 1024
            ),
        )(
            vectors,
            h_tiles.reshape(hq, T, T),
            h_list,
            j_tiles.reshape(jq, T, T),
            j_list,
        )

    return jax.shard_map(
        per_device,
        mesh=mesh,
        in_specs=(
            P(None, None, ("col", "row")),
            P(None, "row", "col", None, None),
            P(None, "row", "col"),
            P(None, "row", "col", None, None),
            P(None, "row", "col"),
        ),
        out_specs=(P(None, None, ("row", "col")), P()),
        check_vma=False,
    )
```

```python
import functools

import jax
import jax.numpy as jnp
from jax import lax
from jax.experimental import pallas as pl
from jax.experimental.pallas import tpu as pltpu
from jax.sharding import PartitionSpec as P

NSIT = 6
MESH = pl.DeviceIdType.MESH
F32 = jnp.float32
BF16 = jnp.bfloat16
NY = 8
NZ = 4
NX = 4
FAR_FIRST = (4, 3, 5, 2, 6, 1, 7)
VEC, HY, JY, JZ, PZ, GA, CA, GB, CB, HU, JU = range(11)
K = 16
T = 128
NT = (((1,), (1,)), ((), ()))


def iota(shape, dim):
    return lax.broadcasted_iota(jnp.int32, shape, dim)


def three_parts(x):
    a = x.astype(BF16).astype(F32)
    rest = x - a
    b = rest.astype(BF16).astype(F32)
    return a, b, rest - b


def small_dot(left, right, group):
    a1, a2, a3 = three_parts(left)
    b1, b2, b3 = (b.astype(BF16) for b in three_parts(right))
    lhs = jnp.where(
        (group == 0) | (group == 1) | (group == 4),
        a1,
        jnp.where((group == 5) | (group == 7), a3, a2),
    )
    rhs = jnp.concatenate([b1, b2, b1, b2, b3, b1, b3, b2], axis=0)
    return jnp.dot(lhs.astype(BF16), rhs, preferred_element_type=F32)


def long_dot(left, right):
    return lax.dot_general(
        left, right, NT, precision=lax.Precision.HIGHEST, preferred_element_type=F32
    )


def coded(piece, first):
    top = jnp.max(jnp.abs(piece), axis=1, keepdims=True)
    unit = (jnp.maximum(top, 1e-30) * (1.01 / 32767)).astype(BF16).astype(F32)
    steps = piece * jnp.broadcast_to(1.0 / unit, (K, T))
    steps = (steps + jnp.where(steps >= 0, 0.5, -0.5)).astype(jnp.int32).astype(jnp.int16)
    place = iota((K, T), 1) == iota((K, T), 0) + first
    units = jnp.sum(
        jnp.where(place, jnp.broadcast_to(unit, (K, T)), 0.0), axis=0, keepdims=True
    )
    return steps, units


def spread_units(units, rows, count):
    own = iota((rows, T), 1) == iota((rows, T), 0)
    placed = jnp.concatenate(
        [
            jnp.where(own, jnp.broadcast_to(units[d], (rows, T)), 0.0).astype(BF16)
            for d in range(count)
        ],
        axis=0,
    )
    return jnp.dot(placed, jnp.ones((T, T), BF16), preferred_element_type=F32)


def decoded_total(steps, unit, rows, count):
    parts = [
        steps[d].astype(jnp.int32).astype(F32) * unit[d * rows : (d + 1) * rows]
        for d in range(count)
    ]
    while len(parts) > 1:
        parts = [parts[k] + parts[k + 1] for k in range(0, len(parts), 2)]
    return parts[0]


def flat_rows(repeated):
    own = iota((8, T), 1) // K == iota((8, T), 0)
    return [
        jnp.sum(jnp.where(own, repeated[8 * h : 8 * h + 8], 0.0), axis=0, keepdims=True)
        for h in range(2)
    ]


def from_flat(rows):
    own = iota((8, T), 1) // K == iota((8, T), 0)
    full = jnp.concatenate(
        [jnp.where(own, jnp.broadcast_to(row, (8, T)), 0.0) for row in rows], axis=0
    )
    for shift in (64, 32, 16):
        full = full + pltpu.roll(full, shift, 1)
    return full


def kernel(
    n_row, n_col, total_rows,
    vec_hbm, ht_hbm, hl_hbm, jt_hbm, jl_hbm, basis_ref, elem_ref,
    vloc, vsend, vrecv, vblk, ht, jt, hl, jl, hs, hr, js, jr, hsu, hru, jsu, jru, jz, pz, gs, ga, gb, cs, ca, cb,
    lsem, ssem, rsem, ready,
):
    me_r = lax.axis_index("row")
    me_c = lax.axis_index("col")
    zh = me_c // NY
    y = me_c % NY
    x = me_r // (n_row // NX)
    inner = me_r % (n_row // NX)
    n_in = n_row // NX
    last = NZ - 1
    at_last = zh == last
    barrier = pltpu.get_barrier_semaphore()

    def wrap(value, count):
        return jnp.where(value >= count, value - count, value)

    def at_row(d):
        return {"row": wrap(me_r + d, n_row)}

    def at_y(d):
        return {"col": zh * NY + wrap(y + d, NY)}

    def at_z(d):
        return {"col": wrap(zh + d, NZ) * NY + y}

    def at_plane(d):
        to = y * NX + x + d
        to = wrap(to, NX * NY)
        return {"row": (to % NX) * n_in + inner, "col": zh * NY + to // NX}

    def at_line(d):
        to = wrap(zh * n_in + inner + d, NZ * n_in)
        return {"row": x * n_in + to % n_in, "col": (to // n_in) * NY + y}

    def at_collector(d):
        return {"col": last * NY + wrap(y + d, NY)}

    codes = [
        pltpu.make_async_copy(hl_hbm, hl, lsem.at[3]),
        pltpu.make_async_copy(jl_hbm, jl, lsem.at[4]),
    ]
    loads = [
        pltpu.make_async_copy(vec_hbm, vloc, lsem.at[0]),
        pltpu.make_async_copy(ht_hbm, ht, lsem.at[1]),
        pltpu.make_async_copy(jt_hbm, jt, lsem.at[2]),
    ]

    def greet(where):
        def step(d, carry):
            pl.semaphore_signal(barrier, inc=1, device_id=where(d), device_id_type=MESH)
            return carry
        return step

    def send_all(at, where, count, src, dst, order=None):
        def step(d, carry):
            pltpu.make_async_remote_copy(
                src_ref=src(d), dst_ref=dst, send_sem=ssem.at[at], recv_sem=rsem.at[at],
                device_id=where(d), device_id_type=MESH,
            ).start()
            return carry
        if order is None:
            lax.fori_loop(1, count + 1, step, 0)
        else:
            for d in order:
                step(d, 0)

    def wait_for(sem, at, buf, count):
        part = buf.at[pl.ds(0, count)]
        pltpu.make_async_copy(part, part, sem.at[at]).wait()

    def total_of(buf, count):
        parts = [buf[d] for d in range(count)]
        while len(parts) > 1:
            parts = [sum(parts[k + 1 : k + 2], parts[k]) for k in range(0, len(parts), 2)]
        return parts[0]

    lax.fori_loop(1, n_row, greet(at_row), 0)
    lax.fori_loop(1, NY, greet(at_y), 0)
    lax.fori_loop(1, NZ, greet(at_z), 0)
    for load in [loads[0]] + codes + loads[1:]:
        load.start()
    loads[0].wait()
    place = (iota((32, T), 1) == iota((32, T), 0) + 32 * lax.rem(me_r, 4)).astype(F32).astype(BF16)
    mine = jnp.dot(vloc[0], place, preferred_element_type=F32).astype(BF16)
    vsend[...] = mine
    vrecv[me_r] = mine
    for load in codes:
        load.wait()

    pl.semaphore_wait(barrier, n_row - 1 + NY - 1 + NZ - 1)
    @pl.when(at_last)
    def _():
        for d in range(1, NZ):
            pl.semaphore_signal(ready, inc=1, device_id=at_z(d), device_id_type=MESH)

    send_all(VEC, at_row, n_row - 1, lambda d: vsend, vrecv.at[me_r])
    loads[1].wait()
    loads[2].wait()
    wait_for(rsem, VEC, vrecv, n_row - 1)

    for c in range(6):
        block = (vrecv[4 * c].astype(F32) + vrecv[4 * c + 1].astype(F32)) + (
            vrecv[4 * c + 2].astype(F32) + vrecv[4 * c + 3].astype(F32)
        )
        vblk[c] = block

    def masked(code, blocks):
        m = lax.shift_right_arithmetic(code * 43, 8)
        picked = vblk[code - 6 * m]
        which = jnp.full((K, T), m, jnp.int32)
        return jnp.concatenate(
            [jnp.where(which == b, picked, 0.0).astype(BF16) for b in range(blocks)], axis=0
        )

    def products(codes, tiles, count, blocks):
        total = jnp.zeros((blocks * K, T), F32)
        for q in range(0, count, 2):
            left = jnp.concatenate([masked(codes[0, 0, q + e], blocks) for e in range(2)], axis=1)
            right = jnp.concatenate([tiles[q + e] for e in range(2)], axis=1)
            total = total + lax.dot_general(left, right, NT, preferred_element_type=F32)
        return total

    lane32 = iota((K, T), 1) // 32

    def packed(total, first, yh, s):
        out = None
        for z in range(NZ):
            at = (first + 2 * z + yh) * K
            piece = total[at : at + K]
            shift = ((z - s) % NZ) * 32
            if shift:
                piece = pltpu.roll(piece, shift, 1)
            out = piece if out is None else jnp.where(lane32 == z, piece, out)
        return out

    j_total = products(jl, jt, jt.shape[0], 16)
    for yh in range(2):
        for s in range(4):
            first, first_units = coded(packed(j_total, 0, yh, s), 0)
            second, second_units = coded(packed(j_total, 8, yh, s), K)
            js[yh * 4 + s, :K] = first
            js[yh * 4 + s, K:] = second
            jsu[yh * 4 + s] = first_units + second_units
    jr[y] = js[y]
    jru[y] = jsu[y]
    send_all(JU, at_y, NY - 1, lambda d: jsu.at[wrap(y + d, NY)], jru.at[y], FAR_FIRST)
    send_all(JY, at_y, NY - 1, lambda d: js.at[wrap(y + d, NY)], jr.at[y], FAR_FIRST)
    h_total = products(hl, ht, ht.shape[0], 8)
    for yh in range(2):
        for s in range(4):
            hs[yh * 4 + s], hsu[yh * 4 + s] = coded(packed(h_total, 0, yh, s), 0)

    def decode_j():
        wait_for(rsem, JU, jru, NY - 1)
        unit = spread_units(jru, 2 * K, NY)
        wait_for(rsem, JY, jr, NY - 1)
        jz[zh] = decoded_total(jr, unit, 2 * K, NY)

    @pl.when(jnp.logical_not(at_last))
    def _():
        pl.semaphore_wait(ready, 1)
        send_all(
            HU, at_collector, NY, lambda d: hsu.at[wrap(y + d, NY)], hru.at[me_c], FAR_FIRST + (0,)
        )
        send_all(
            HY, at_collector, NY, lambda d: hs.at[wrap(y + d, NY)], hr.at[me_c], FAR_FIRST + (0,)
        )
        decode_j()
        send_all(JZ, lambda d: at_collector(0), 1, lambda d: jz.at[zh], jz.at[zh])
        wait_for(rsem, PZ, pz, 1)
        wait_for(rsem, GB, gb, n_in)

    @pl.when(at_last)
    def _():
        slot = y * NX + x
        hr[me_c] = hs[y]
        hru[me_c] = hsu[y]
        send_all(
            HU, at_collector, NY - 1, lambda d: hsu.at[wrap(y + d, NY)], hru.at[me_c], FAR_FIRST
        )
        send_all(
            HY, at_collector, NY - 1, lambda d: hs.at[wrap(y + d, NY)], hr.at[me_c], FAR_FIRST
        )
        decode_j()
        wait_for(rsem, HU, hru, n_col - 1)
        unit = spread_units(hru, K, n_col)
        wait_for(rsem, HY, hr, n_col - 1)
        proj = decoded_total(hr, unit, K, n_col)
        pz[0] = proj
        rows = flat_rows(long_dot(proj, jnp.concatenate([proj] * 8, axis=0)))
        for h in range(2):
            gs[h : h + 1] = rows[h]
            ga[slot, h : h + 1] = rows[h]
        send_all(GA, at_plane, NX * NY - 1, lambda d: gs, ga.at[slot])
        send_all(PZ, at_z, NZ - 1, lambda d: pz.at[0], pz.at[0])

        wait_for(rsem, JZ, jz, NZ - 1)
        share = total_of(jz, NZ)
        for o in range(2):
            rows = flat_rows(
                long_dot(proj, jnp.concatenate([share[o * K : o * K + K]] * 8, axis=0))
            )
            for h in range(2):
                cs[2 * o + h : 2 * o + h + 1] = rows[h]
                ca[slot, 2 * o + h : 2 * o + h + 1] = rows[h]
        send_all(CA, at_plane, NX * NY - 1, lambda d: cs, ca.at[slot])

        wait_for(rsem, GA, ga, NX * NY - 1)
        gb[inner] = total_of(ga, NX * NY)
        send_all(GB, at_line, NZ * n_in - 1, lambda d: gb.at[inner], gb.at[inner])
        wait_for(rsem, CA, ca, NX * NY - 1)
        cb[inner] = total_of(ca, NX * NY)
        send_all(CB, at_line, NZ * n_in - 1, lambda d: cb.at[inner], cb.at[inner])
        wait_for(rsem, GB, gb, n_in - 1)

    part = total_of(gb, n_in)
    square = jnp.sum(jnp.sum(part * part, axis=1, keepdims=True), axis=0, keepdims=True)
    scale = jnp.sqrt(jnp.broadcast_to(square, (K, T)) + 1e-06)
    iterate = from_flat([part[0:1], part[1:2]]) / scale
    group = iota((K, T), 1) // K
    identity = (iota((K, T), 1) % K == iota((K, T), 0)).astype(F32)
    middle = 1.5 * identity - 0.5 * iterate
    iterate = small_dot(middle, iterate, group)
    root = middle
    for step in range(1, NSIT):
        middle = 1.5 * identity - 0.5 * small_dot(iterate, root, group)
        if step < NSIT - 1:
            iterate = small_dot(middle, iterate, group)
        root = small_dot(root, middle, group)
    basis = jnp.sqrt(total_rows / scale) * small_dot(root, pz[0], group)
    own_lanes = basis
    for z in range(1, NZ):
        own_lanes = jnp.where(
            jnp.full((K, T), zh, jnp.int32) == z, pltpu.roll(basis, (NZ - z) * 32, 1), own_lanes
        )
    basis_ref[0] = own_lanes[:, :32]

    scaled = root / jnp.sqrt(scale)

    @pl.when(jnp.logical_not(at_last))
    def _():
        wait_for(rsem, CB, cb, n_in)

    @pl.when(at_last)
    def _():
        wait_for(rsem, CB, cb, n_in - 1)

    part = total_of(cb, n_in)
    for o in range(2):
        cross = from_flat([part[2 * o : 2 * o + 1], part[2 * o + 1 : 2 * o + 2]])
        elem_ref[0, o] = small_dot(scaled, cross, group)[:, :K]

    @pl.when(jnp.logical_not(at_last))
    def _():
        wait_for(ssem, HU, hru, NY)
        wait_for(ssem, HY, hr, NY)
        wait_for(ssem, JZ, jz, 1)

    @pl.when(at_last)
    def _():
        wait_for(ssem, HU, hru, NY - 1)
        wait_for(ssem, HY, hr, NY - 1)
        wait_for(ssem, GA, ga, NX * NY - 1)
        for _ in range(NZ - 1):
            wait_for(ssem, PZ, pz, 1)
        wait_for(ssem, CA, ca, NX * NY - 1)
        for at, buf in ((GB, gb), (CB, cb)):
            for _ in range(NZ - 1):
                wait_for(ssem, at, buf, n_in)
            wait_for(ssem, at, buf, n_in - 1)

    wait_for(ssem, VEC, vrecv, n_row - 1)
    wait_for(ssem, JU, jru, NY - 1)
    wait_for(ssem, JY, jr, NY - 1)


def solution(mesh):
    n_row, n_col = mesh.shape["row"], mesh.shape["col"]

    def per_device(vectors, h_tiles, h_list, j_tiles, j_list):
        hq, jq = h_tiles.shape[2], j_tiles.shape[2]
        total_rows = vectors.shape[2] * n_row * n_col
        hbm = pl.BlockSpec(memory_space=pltpu.HBM)
        vmem = pl.BlockSpec(memory_space=pltpu.VMEM)
        return pl.pallas_call(
            functools.partial(kernel, n_row, n_col, float(total_rows)),
            out_shape=(
                pltpu.VMEM((1, K, 32), F32),
                pltpu.VMEM((1, 2, K, K), F32),
            ),
            in_specs=[hbm] * 5,
            out_specs=(vmem, vmem),
            scratch_shapes=[
                pltpu.VMEM((1, K, 32), BF16),
                pltpu.VMEM((K, T), BF16),
                pltpu.VMEM((n_row, K, T), BF16),
                pltpu.VMEM((6, K, T), F32),
                pltpu.VMEM((hq, T, T), BF16),
                pltpu.VMEM((jq, T, T), BF16),
                pltpu.SMEM((1, 1, hq), jnp.int32),
                pltpu.SMEM((1, 1, jq), jnp.int32),
                pltpu.VMEM((NY, K, T), jnp.int16),
                pltpu.VMEM((n_col, K, T), jnp.int16),
                pltpu.VMEM((NY, 2 * K, T), jnp.int16),
                pltpu.VMEM((NY, 2 * K, T), jnp.int16),
                pltpu.VMEM((NY, 1, T), F32),
                pltpu.VMEM((n_col, 1, T), F32),
                pltpu.VMEM((NY, 1, T), F32),
                pltpu.VMEM((NY, 1, T), F32),
                pltpu.VMEM((NZ, 2 * K, T), F32),
                pltpu.VMEM((1, K, T), F32),
                pltpu.VMEM((2, T), F32),
                pltpu.VMEM((NX * NY, 2, T), F32),
                pltpu.VMEM((n_row // NX, 2, T), F32),
                pltpu.VMEM((4, T), F32),
                pltpu.VMEM((NX * NY, 4, T), F32),
                pltpu.VMEM((n_row // NX, 4, T), F32),
                pltpu.SemaphoreType.DMA((5,)),
                pltpu.SemaphoreType.DMA((12,)),
                pltpu.SemaphoreType.DMA((12,)),
                pltpu.SemaphoreType.REGULAR,
            ],
            compiler_params=pltpu.CompilerParams(
                collective_id=0, has_side_effects=True, vmem_limit_bytes=60 * 1024 * 1024
            ),
        )(
            vectors,
            h_tiles.reshape(hq, T, T),
            h_list,
            j_tiles.reshape(jq, T, T),
            j_list,
        )

    return jax.shard_map(
        per_device,
        mesh=mesh,
        in_specs=(
            P(None, None, ("col", "row")),
            P(None, "row", "col", None, None),
            P(None, "row", "col"),
            P(None, "row", "col", None, None),
            P(None, "row", "col"),
        ),
        out_specs=(P(None, None, ("row", "col")), P()),
        check_vma=False,
    )
```

```python
import functools

import jax
import jax.numpy as jnp
from jax import lax
from jax.experimental import pallas as pl
from jax.experimental.pallas import tpu as pltpu
from jax.sharding import PartitionSpec as P

NSIT = 6
MESH = pl.DeviceIdType.MESH
F32 = jnp.float32
BF16 = jnp.bfloat16
NY = 8
NZ = 4
NX = 4
FAR_FIRST = (4, 3, 5, 2, 6, 1, 7)
VEC, HY, JY, JZ, PZ, GA, CA, GB, CB, HU, JU = range(11)
K = 16
T = 128
NT = (((1,), (1,)), ((), ()))


def iota(shape, dim):
    return lax.broadcasted_iota(jnp.int32, shape, dim)


def three_parts(x):
    a = x.astype(BF16).astype(F32)
    rest = x - a
    b = rest.astype(BF16).astype(F32)
    return a, b, rest - b


def small_dot(left, right, group):
    a1, a2, a3 = three_parts(left)
    b1, b2, b3 = (b.astype(BF16) for b in three_parts(right))
    lhs = jnp.where(
        (group == 0) | (group == 1) | (group == 4),
        a1,
        jnp.where((group == 5) | (group == 7), a3, a2),
    )
    rhs = jnp.concatenate([b1, b2, b1, b2, b3, b1, b3, b2], axis=0)
    return jnp.dot(lhs.astype(BF16), rhs, preferred_element_type=F32)


def long_dot(left, right):
    return lax.dot_general(
        left, right, NT, precision=lax.Precision.HIGHEST, preferred_element_type=F32
    )


def coded(piece, first):
    top = jnp.max(jnp.abs(piece), axis=1, keepdims=True)
    unit = (jnp.maximum(top, 1e-30) * (1.01 / 32767)).astype(BF16).astype(F32)
    steps = piece * jnp.broadcast_to(1.0 / unit, (K, T))
    steps = (steps + jnp.where(steps >= 0, 0.5, -0.5)).astype(jnp.int32).astype(jnp.int16)
    place = iota((K, T), 1) == iota((K, T), 0) + first
    units = jnp.sum(
        jnp.where(place, jnp.broadcast_to(unit, (K, T)), 0.0), axis=0, keepdims=True
    )
    return steps, units


def spread_units(units, rows, count):
    own = iota((rows, T), 1) == iota((rows, T), 0)
    placed = jnp.concatenate(
        [
            jnp.where(own, jnp.broadcast_to(units[d], (rows, T)), 0.0).astype(BF16)
            for d in range(count)
        ],
        axis=0,
    )
    return jnp.dot(placed, jnp.ones((T, T), BF16), preferred_element_type=F32)


def decoded_total(steps, unit, rows, count):
    parts = [
        steps[d].astype(jnp.int32).astype(F32) * unit[d * rows : (d + 1) * rows]
        for d in range(count)
    ]
    while len(parts) > 1:
        parts = [parts[k] + parts[k + 1] for k in range(0, len(parts), 2)]
    return parts[0]


def flat_rows(repeated):
    own = iota((8, T), 1) // K == iota((8, T), 0)
    return [
        jnp.sum(jnp.where(own, repeated[8 * h : 8 * h + 8], 0.0), axis=0, keepdims=True)
        for h in range(2)
    ]


def from_flat(rows):
    own = iota((8, T), 1) // K == iota((8, T), 0)
    full = jnp.concatenate(
        [jnp.where(own, jnp.broadcast_to(row, (8, T)), 0.0) for row in rows], axis=0
    )
    for shift in (64, 32, 16):
        full = full + pltpu.roll(full, shift, 1)
    return full


def kernel(
    n_row, n_col, total_rows,
    vec_hbm, ht_hbm, hl_hbm, jt_hbm, jl_hbm, basis_ref, elem_ref,
    vloc, vsend, vrecv, vblk, ht, jt, hl, jl, hs, hr, js, jr, hsu, hru, jsu, jru, jz, pz, gs, ga, gb, cs, ca, cb,
    lsem, ssem, rsem, ready,
):
    me_r = lax.axis_index("row")
    me_c = lax.axis_index("col")
    zh = me_c // NY
    y = me_c % NY
    x = me_r // (n_row // NX)
    inner = me_r % (n_row // NX)
    n_in = n_row // NX
    last = NZ - 1
    at_last = zh == last
    barrier = pltpu.get_barrier_semaphore()

    def wrap(value, count):
        return jnp.where(value >= count, value - count, value)

    def at_row(d):
        return {"row": wrap(me_r + d, n_row)}

    def at_y(d):
        return {"col": zh * NY + wrap(y + d, NY)}

    def at_z(d):
        return {"col": wrap(zh + d, NZ) * NY + y}

    def at_plane(d):
        to = y * NX + x + 1 + wrap(d + 12, NX * NY - 1)
        to = wrap(to, NX * NY)
        return {"row": (to % NX) * n_in + inner, "col": zh * NY + to // NX}

    def at_line(d):
        to = wrap(zh * n_in + inner + d, NZ * n_in)
        return {"row": x * n_in + to % n_in, "col": (to // n_in) * NY + y}

    def at_collector(d):
        return {"col": last * NY + wrap(y + d, NY)}

    codes = [
        pltpu.make_async_copy(hl_hbm, hl, lsem.at[3]),
        pltpu.make_async_copy(jl_hbm, jl, lsem.at[4]),
    ]
    loads = [
        pltpu.make_async_copy(vec_hbm, vloc, lsem.at[0]),
        pltpu.make_async_copy(ht_hbm, ht, lsem.at[1]),
        pltpu.make_async_copy(jt_hbm, jt, lsem.at[2]),
    ]

    def greet(where):
        def step(d, carry):
            pl.semaphore_signal(barrier, inc=1, device_id=where(d), device_id_type=MESH)
            return carry
        return step

    def send_all(at, where, count, src, dst, order=None):
        def step(d, carry):
            pltpu.make_async_remote_copy(
                src_ref=src(d), dst_ref=dst, send_sem=ssem.at[at], recv_sem=rsem.at[at],
                device_id=where(d), device_id_type=MESH,
            ).start()
            return carry
        if order is None:
            lax.fori_loop(1, count + 1, step, 0)
        else:
            for d in order:
                step(d, 0)

    def wait_for(sem, at, buf, count):
        part = buf.at[pl.ds(0, count)]
        pltpu.make_async_copy(part, part, sem.at[at]).wait()

    def total_of(buf, count):
        parts = [buf[d] for d in range(count)]
        while len(parts) > 1:
            parts = [sum(parts[k + 1 : k + 2], parts[k]) for k in range(0, len(parts), 2)]
        return parts[0]

    lax.fori_loop(1, n_row, greet(at_row), 0)
    lax.fori_loop(1, NY, greet(at_y), 0)
    lax.fori_loop(1, NZ, greet(at_z), 0)
    for load in [loads[0]] + codes + loads[1:]:
        load.start()
    loads[0].wait()
    place = (iota((32, T), 1) == iota((32, T), 0) + 32 * lax.rem(me_r, 4)).astype(F32).astype(BF16)
    mine = jnp.dot(vloc[0], place, preferred_element_type=F32).astype(BF16)
    vsend[...] = mine
    vrecv[me_r] = mine
    for load in codes:
        load.wait()

    pl.semaphore_wait(barrier, n_row - 1 + NY - 1 + NZ - 1)
    @pl.when(at_last)
    def _():
        for d in range(1, NZ):
            pl.semaphore_signal(ready, inc=1, device_id=at_z(d), device_id_type=MESH)

    send_all(VEC, at_row, n_row - 1, lambda d: vsend, vrecv.at[me_r])
    loads[1].wait()
    loads[2].wait()
    wait_for(rsem, VEC, vrecv, n_row - 1)

    for c in range(6):
        block = (vrecv[4 * c].astype(F32) + vrecv[4 * c + 1].astype(F32)) + (
            vrecv[4 * c + 2].astype(F32) + vrecv[4 * c + 3].astype(F32)
        )
        vblk[c] = block

    def masked(code, blocks):
        m = lax.shift_right_arithmetic(code * 43, 8)
        picked = vblk[code - 6 * m]
        which = jnp.full((K, T), m, jnp.int32)
        return jnp.concatenate(
            [jnp.where(which == b, picked, 0.0).astype(BF16) for b in range(blocks)], axis=0
        )

    def products(codes, tiles, count, blocks):
        total = jnp.zeros((blocks * K, T), F32)
        for q in range(0, count, 2):
            left = jnp.concatenate([masked(codes[0, 0, q + e], blocks) for e in range(2)], axis=1)
            right = jnp.concatenate([tiles[q + e] for e in range(2)], axis=1)
            total = total + lax.dot_general(left, right, NT, preferred_element_type=F32)
        return total

    lane32 = iota((K, T), 1) // 32

    def packed(total, first, yh, s):
        out = None
        for z in range(NZ):
            at = (first + 2 * z + yh) * K
            piece = total[at : at + K]
            shift = ((z - s) % NZ) * 32
            if shift:
                piece = pltpu.roll(piece, shift, 1)
            out = piece if out is None else jnp.where(lane32 == z, piece, out)
        return out

    j_total = products(jl, jt, jt.shape[0], 16)
    for yh in range(2):
        for s in range(4):
            first, first_units = coded(packed(j_total, 0, yh, s), 0)
            second, second_units = coded(packed(j_total, 8, yh, s), K)
            js[yh * 4 + s, :K] = first
            js[yh * 4 + s, K:] = second
            jsu[yh * 4 + s] = first_units + second_units
    jr[y] = js[y]
    jru[y] = jsu[y]
    send_all(JU, at_y, NY - 1, lambda d: jsu.at[wrap(y + d, NY)], jru.at[y], FAR_FIRST)
    send_all(JY, at_y, NY - 1, lambda d: js.at[wrap(y + d, NY)], jr.at[y], FAR_FIRST)
    h_total = products(hl, ht, ht.shape[0], 8)
    for yh in range(2):
        for s in range(4):
            hs[yh * 4 + s], hsu[yh * 4 + s] = coded(packed(h_total, 0, yh, s), 0)

    def decode_j():
        wait_for(rsem, JU, jru, NY - 1)
        unit = spread_units(jru, 2 * K, NY)
        wait_for(rsem, JY, jr, NY - 1)
        jz[zh] = decoded_total(jr, unit, 2 * K, NY)

    @pl.when(jnp.logical_not(at_last))
    def _():
        pl.semaphore_wait(ready, 1)
        send_all(
            HU, at_collector, NY, lambda d: hsu.at[wrap(y + d, NY)], hru.at[me_c], FAR_FIRST + (0,)
        )
        send_all(
            HY, at_collector, NY, lambda d: hs.at[wrap(y + d, NY)], hr.at[me_c], FAR_FIRST + (0,)
        )
        decode_j()
        send_all(JZ, lambda d: at_collector(0), 1, lambda d: jz.at[zh], jz.at[zh])
        wait_for(rsem, PZ, pz, 1)
        wait_for(rsem, GB, gb, n_in)

    @pl.when(at_last)
    def _():
        slot = y * NX + x
        hr[me_c] = hs[y]
        hru[me_c] = hsu[y]
        send_all(
            HU, at_collector, NY - 1, lambda d: hsu.at[wrap(y + d, NY)], hru.at[me_c], FAR_FIRST
        )
        send_all(
            HY, at_collector, NY - 1, lambda d: hs.at[wrap(y + d, NY)], hr.at[me_c], FAR_FIRST
        )
        decode_j()
        wait_for(rsem, HU, hru, n_col - 1)
        unit = spread_units(hru, K, n_col)
        wait_for(rsem, HY, hr, n_col - 1)
        proj = decoded_total(hr, unit, K, n_col)
        pz[0] = proj
        rows = flat_rows(long_dot(proj, jnp.concatenate([proj] * 8, axis=0)))
        for h in range(2):
            gs[h : h + 1] = rows[h]
            ga[slot, h : h + 1] = rows[h]
        send_all(GA, at_plane, NX * NY - 1, lambda d: gs, ga.at[slot])
        send_all(PZ, at_z, NZ - 1, lambda d: pz.at[0], pz.at[0])

        wait_for(rsem, JZ, jz, NZ - 1)
        share = total_of(jz, NZ)
        for o in range(2):
            rows = flat_rows(
                long_dot(proj, jnp.concatenate([share[o * K : o * K + K]] * 8, axis=0))
            )
            for h in range(2):
                cs[2 * o + h : 2 * o + h + 1] = rows[h]
                ca[slot, 2 * o + h : 2 * o + h + 1] = rows[h]
        send_all(CA, at_plane, NX * NY - 1, lambda d: cs, ca.at[slot])

        wait_for(rsem, GA, ga, NX * NY - 1)
        gb[inner] = total_of(ga, NX * NY)
        send_all(GB, at_line, NZ * n_in - 1, lambda d: gb.at[inner], gb.at[inner])
        wait_for(rsem, CA, ca, NX * NY - 1)
        cb[inner] = total_of(ca, NX * NY)
        send_all(CB, at_line, NZ * n_in - 1, lambda d: cb.at[inner], cb.at[inner])
        wait_for(rsem, GB, gb, n_in - 1)

    part = total_of(gb, n_in)
    square = jnp.sum(jnp.sum(part * part, axis=1, keepdims=True), axis=0, keepdims=True)
    scale = jnp.sqrt(jnp.broadcast_to(square, (K, T)) + 1e-06)
    iterate = from_flat([part[0:1], part[1:2]]) / scale
    group = iota((K, T), 1) // K
    identity = (iota((K, T), 1) % K == iota((K, T), 0)).astype(F32)
    middle = 1.5 * identity - 0.5 * iterate
    iterate = small_dot(middle, iterate, group)
    root = middle
    for step in range(1, NSIT):
        middle = 1.5 * identity - 0.5 * small_dot(iterate, root, group)
        if step < NSIT - 1:
            iterate = small_dot(middle, iterate, group)
        root = small_dot(root, middle, group)
    basis = jnp.sqrt(total_rows / scale) * small_dot(root, pz[0], group)
    own_lanes = basis
    for z in range(1, NZ):
        own_lanes = jnp.where(
            jnp.full((K, T), zh, jnp.int32) == z, pltpu.roll(basis, (NZ - z) * 32, 1), own_lanes
        )
    basis_ref[0] = own_lanes[:, :32]

    scaled = root / jnp.sqrt(scale)

    @pl.when(jnp.logical_not(at_last))
    def _():
        wait_for(rsem, CB, cb, n_in)

    @pl.when(at_last)
    def _():
        wait_for(rsem, CB, cb, n_in - 1)

    part = total_of(cb, n_in)
    for o in range(2):
        cross = from_flat([part[2 * o : 2 * o + 1], part[2 * o + 1 : 2 * o + 2]])
        elem_ref[0, o] = small_dot(scaled, cross, group)[:, :K]

    @pl.when(jnp.logical_not(at_last))
    def _():
        wait_for(ssem, HU, hru, NY)
        wait_for(ssem, HY, hr, NY)
        wait_for(ssem, JZ, jz, 1)

    @pl.when(at_last)
    def _():
        wait_for(ssem, HU, hru, NY - 1)
        wait_for(ssem, HY, hr, NY - 1)
        wait_for(ssem, GA, ga, NX * NY - 1)
        for _ in range(NZ - 1):
            wait_for(ssem, PZ, pz, 1)
        wait_for(ssem, CA, ca, NX * NY - 1)
        for at, buf in ((GB, gb), (CB, cb)):
            for _ in range(NZ - 1):
                wait_for(ssem, at, buf, n_in)
            wait_for(ssem, at, buf, n_in - 1)

    wait_for(ssem, VEC, vrecv, n_row - 1)
    wait_for(ssem, JU, jru, NY - 1)
    wait_for(ssem, JY, jr, NY - 1)


def solution(mesh):
    n_row, n_col = mesh.shape["row"], mesh.shape["col"]

    def per_device(vectors, h_tiles, h_list, j_tiles, j_list):
        hq, jq = h_tiles.shape[2], j_tiles.shape[2]
        total_rows = vectors.shape[2] * n_row * n_col
        hbm = pl.BlockSpec(memory_space=pltpu.HBM)
        vmem = pl.BlockSpec(memory_space=pltpu.VMEM)
        return pl.pallas_call(
            functools.partial(kernel, n_row, n_col, float(total_rows)),
            out_shape=(
                pltpu.VMEM((1, K, 32), F32),
                pltpu.VMEM((1, 2, K, K), F32),
            ),
            in_specs=[hbm] * 5,
            out_specs=(vmem, vmem),
            scratch_shapes=[
                pltpu.VMEM((1, K, 32), BF16),
                pltpu.VMEM((K, T), BF16),
                pltpu.VMEM((n_row, K, T), BF16),
                pltpu.VMEM((6, K, T), F32),
                pltpu.VMEM((hq, T, T), BF16),
                pltpu.VMEM((jq, T, T), BF16),
                pltpu.SMEM((1, 1, hq), jnp.int32),
                pltpu.SMEM((1, 1, jq), jnp.int32),
                pltpu.VMEM((NY, K, T), jnp.int16),
                pltpu.VMEM((n_col, K, T), jnp.int16),
                pltpu.VMEM((NY, 2 * K, T), jnp.int16),
                pltpu.VMEM((NY, 2 * K, T), jnp.int16),
                pltpu.VMEM((NY, 1, T), F32),
                pltpu.VMEM((n_col, 1, T), F32),
                pltpu.VMEM((NY, 1, T), F32),
                pltpu.VMEM((NY, 1, T), F32),
                pltpu.VMEM((NZ, 2 * K, T), F32),
                pltpu.VMEM((1, K, T), F32),
                pltpu.VMEM((2, T), F32),
                pltpu.VMEM((NX * NY, 2, T), F32),
                pltpu.VMEM((n_row // NX, 2, T), F32),
                pltpu.VMEM((4, T), F32),
                pltpu.VMEM((NX * NY, 4, T), F32),
                pltpu.VMEM((n_row // NX, 4, T), F32),
                pltpu.SemaphoreType.DMA((5,)),
                pltpu.SemaphoreType.DMA((12,)),
                pltpu.SemaphoreType.DMA((12,)),
                pltpu.SemaphoreType.REGULAR,
            ],
            compiler_params=pltpu.CompilerParams(
                collective_id=0, has_side_effects=True, vmem_limit_bytes=60 * 1024 * 1024
            ),
        )(
            vectors,
            h_tiles.reshape(hq, T, T),
            h_list,
            j_tiles.reshape(jq, T, T),
            j_list,
        )

    return jax.shard_map(
        per_device,
        mesh=mesh,
        in_specs=(
            P(None, None, ("col", "row")),
            P(None, "row", "col", None, None),
            P(None, "row", "col"),
            P(None, "row", "col", None, None),
            P(None, "row", "col"),
        ),
        out_specs=(P(None, None, ("row", "col")), P()),
        check_vma=False,
    )
```
